128 devices in a mesh: seq: 32 (over z, x, core), tp: 4 (over y).
Axes of the slice: x: 4, y: 4, z: 4, core: 2. Of those that a mesh axis runs over, the one named last changes fastest.
Arguments:
- tokens: bfloat16 [8192, 5120], P('seq', 'tp'), may hold values from -21 to 21
- w_query: bfloat16 [5120, 2560], P(None, 'tp'), may hold values from -1.1 to 1.1
- b_query: bfloat16 [2560], P('tp'), may hold values from -3 to 3
- w_key: bfloat16 [5120, 512], P(None, 'tp'), may hold values from -1.1 to 1.1
- key_bias: bfloat16 [512], P('tp'), may hold values from -3 to 3
- value_weight: bfloat16 [5120, 512], P(None, 'tp'), may hold values from -0.078125 to 0.078125
- value_bias: bfloat16 [512], P('tp'), may hold values from -3 to 3
- w_out: bfloat16 [2560, 5120], P('tp'), may hold values from -0.5 to 0.5
- doc_lengths: int32 [4], replicated, may hold values from 1 to 4096, 8192 in all
- grad_out: bfloat16 [8192, 5120], P('seq', 'tp'), may hold values from -1.1953125 to 1.1953125
Outputs:
- output: bfloat16 [8192, 5120], P('seq', 'tp')
- grad_tokens: bfloat16 [8192, 5120], P('seq', 'tp')
The draws below stay inside these ranges and needn't reach their ends.
All inputs are finite; a program needn't handle non-finite values.
Results may differ from the reference program's by a relative error of at most 0.025.
Values may be sent and summed in bfloat16 or wider, within the bound.
A program may use at most 128 MiB of HBM per device.

```python
import math
import jax
import jax.numpy as jnp
import numpy as np
from jax import lax

MODEL_WIDTH = 5120
QUERY_HEADS = 20
KEY_VALUE_HEADS = 4
HEAD_SIZE = 128
DOCS = 4
TOKENS = 8192
MOST = 4096


def projected_input(key, local_key, width):
    spread = (2.0 / MODEL_WIDTH) ** 0.5
    values = jnp.clip(jax.random.normal(local_key, (MODEL_WIDTH, width), jnp.float32), -6.0, 6.0) * spread
    return values.astype(jnp.bfloat16)


def draw_w_query(key, part):
    local_key = jax.random.fold_in(key, 21)
    return projected_input(key, local_key, QUERY_HEADS * HEAD_SIZE)


def draw_w_key(key, part):
    local_key = jax.random.fold_in(key, 22)
    return projected_input(key, local_key, KEY_VALUE_HEADS * HEAD_SIZE)


def draw_tokens(key, part):
    local_key = jax.random.fold_in(key, 11)
    base_key = jax.random.fold_in(local_key, 0)
    values = jnp.clip(jax.random.normal(base_key, (TOKENS, MODEL_WIDTH), jnp.float32), -6.0, 6.0)
    return values.astype(jnp.bfloat16)


def levels(own_key, dims, pieces, least, largest):
    gain = 1.0
    for axis_at, shards_of in pieces:
        steps = jax.random.uniform(jax.random.fold_in(jax.random.fold_in(own_key, 6), axis_at), (shards_of,), jnp.float32, least / len(pieces), largest / len(pieces))
        gain = gain * jnp.repeat(jnp.exp(steps), dims[axis_at] // shards_of).reshape((-1,) + (1,) * (len(dims) - 1 - axis_at))
    return gain


def profile(number_of, total, limit, lean):
    weights = [(1 << 20) // math.isqrt(rank ** lean) + 1 for rank in range(2, number_of + 1)]
    rest, holding = total - limit - (number_of - 1), [1] * (number_of - 1)
    while rest > 0:
        movable = [i for i in range(number_of - 1) if holding[i] < limit]
        mass, left = sum([weights[i] for i in movable]), rest
        for i in movable:
            addition = min(limit - holding[i], max(1, left * weights[i] // mass), rest)
            holding[i] = holding[i] + addition
            rest = rest - addition
    return np.array([limit] + holding)


def ragged_sizes(own_key, count, total, limit, skew):
    if count == 2:
        one = jax.random.randint(own_key, (), max(1, total - limit), min(limit, total - 1) + 1)
        return jnp.stack([one, total - one])
    lengths = jnp.asarray(profile(count, total, limit, skew), jnp.int32)
    couples = (count - 1) // 2
    donor, sink = lengths[1:1 + 2 * couples:2], lengths[2:2 + 2 * couples:2]
    slack = jnp.minimum(donor - 1, limit - sink)
    shifted = jax.random.randint(jax.random.fold_in(own_key, 1), (couples,), 0, 1 << 20) % (slack + 1)
    lengths = lengths.at[1:1 + 2 * couples:2].set(donor - shifted).at[2:2 + 2 * couples:2].set(sink + shifted)
    return lengths[jax.random.permutation(jax.random.fold_in(own_key, 2), count)]


def normal_values(stream_key, shape, deviation, bound, pieces=(), held_as=jnp.bfloat16):
    result = jax.random.normal(stream_key, shape, jnp.float32) * deviation
    if len(pieces) > 0:
        result = levels(stream_key, shape, pieces, -0.22, 0.18) * result
    return jnp.clip(result, min=-bound, max=bound).astype(held_as)


def setup_inputs(seed: int = 0) -> dict:
    seeds = jax.random.split(jax.random.key(seed), 11)
    tokens = draw_tokens(jax.random.fold_in(seeds[10], 71), 0)
    w_query = draw_w_query(jax.random.fold_in(seeds[10], 71), 0)
    b_query = normal_values(seeds[2], (QUERY_HEADS * HEAD_SIZE,), 0.5, 3.0, ((0, 4),))
    w_key = draw_w_key(jax.random.fold_in(seeds[10], 71), 0)
    key_bias = normal_values(seeds[4], (KEY_VALUE_HEADS * HEAD_SIZE,), 0.5, 3.0, ((0, 4),))
    value_weight = normal_values(seeds[5], (MODEL_WIDTH, KEY_VALUE_HEADS * HEAD_SIZE), MODEL_WIDTH ** -0.5, 0.078125, ((1, 4),))
    value_bias = normal_values(seeds[6], (KEY_VALUE_HEADS * HEAD_SIZE,), 0.5, 3.0, ((0, 4),))
    w_out = normal_values(seeds[7], (QUERY_HEADS * HEAD_SIZE, MODEL_WIDTH), (QUERY_HEADS * HEAD_SIZE // 16) ** -0.5, 0.5, ((0, 4),))
    doc_lengths = ragged_sizes(seeds[8], DOCS, TOKENS, MOST, 1).astype(jnp.int32)
    grad_out = normal_values(seeds[9], (TOKENS, MODEL_WIDTH), 0.2, 1.1953125, ((0, 32), (1, 4)))
    return dict(tokens=tokens, w_query=w_query, b_query=b_query, w_key=w_key, key_bias=key_bias, value_weight=value_weight, value_bias=value_bias, w_out=w_out, doc_lengths=doc_lengths, grad_out=grad_out)


theta_base = 1000000.0
neg_large = -1.0e30


def doc_bounds(doc_lengths):
    doc_ends = jnp.cumsum(doc_lengths).astype(jnp.int32)
    return doc_ends - doc_lengths, doc_ends


def start_of(token_index, doc_starts, doc_ends):
    inside = (token_index[:, None] >= doc_starts[None, :]) & (token_index[:, None] < doc_ends[None, :])
    return jnp.sum(jnp.where(inside, doc_starts[None, :], 0), axis=1).astype(jnp.int32)


def rope_tables(position, head_dim):
    halfway = head_dim // 2
    frequency = theta_base ** (-2.0 * jnp.arange(halfway, dtype=jnp.float32) / head_dim)
    angles = position.astype(jnp.float32)[:, None] * frequency[None, :]
    return jnp.cos(angles)[:, None, :], jnp.sin(angles)[:, None, :]


def apply_rotation(values, cosine_table, sine_table):
    halfway = values.shape[-1] // 2
    former = values[..., :halfway]
    latter = values[..., halfway:]
    return jnp.concatenate([former * cosine_table - latter * sine_table, latter * cosine_table + former * sine_table], axis=-1)


def inverse_rotation(values, cosine_table, sine_table):
    halfway = values.shape[-1] // 2
    former = values[..., :halfway]
    latter = values[..., halfway:]
    return jnp.concatenate([former * cosine_table + latter * sine_table, latter * cosine_table - former * sine_table], axis=-1)


def allowed_mask(row_index, row_start, col_index, col_start):
    return (col_index[None, :] <= row_index[:, None]) & (col_start[None, :] == row_start[:, None])


def rounded(values):
    return lax.optimization_barrier(values.astype(jnp.bfloat16)).astype(jnp.float32)


def reference(tokens, w_query, b_query, w_key, key_bias, value_weight, value_bias, w_out, doc_lengths, grad_out):
    token_total_count = tokens.shape[0]
    query_groups = QUERY_HEADS // KEY_VALUE_HEADS
    factor = HEAD_SIZE ** -0.5
    doc_starts, doc_ends = doc_bounds(doc_lengths)
    token_index = jnp.arange(token_total_count, dtype=jnp.int32)
    token_start = start_of(token_index, doc_starts, doc_ends)
    cosine_table, sine_table = rope_tables(token_index - token_start, HEAD_SIZE)
    query_raw = jnp.dot(tokens, w_query, preferred_element_type=jnp.float32) + b_query.astype(jnp.float32)
    query_matrix = apply_rotation(query_raw.reshape(token_total_count, QUERY_HEADS, HEAD_SIZE), cosine_table, sine_table).astype(jnp.bfloat16)
    key_unrotated = jnp.dot(tokens, w_key, preferred_element_type=jnp.float32) + key_bias.astype(jnp.float32)
    every_key = apply_rotation(key_unrotated.reshape(token_total_count, KEY_VALUE_HEADS, HEAD_SIZE), cosine_table, sine_table).astype(jnp.bfloat16)
    value_unprojected = jnp.dot(tokens, value_weight, preferred_element_type=jnp.float32) + value_bias.astype(jnp.float32)
    every_value = value_unprojected.reshape(token_total_count, KEY_VALUE_HEADS, HEAD_SIZE).astype(jnp.bfloat16)
    query_function = query_matrix.astype(jnp.float32).reshape(token_total_count, KEY_VALUE_HEADS, query_groups, HEAD_SIZE)
    key_f = every_key.astype(jnp.float32)
    value_f = every_value.astype(jnp.float32)
    span_rows = 512 if token_total_count % 512 == 0 else token_total_count

    def block_scores(begin_row):
        low_key = max(0, begin_row - MOST)
        high_key = begin_row + span_rows
        allowed = allowed_mask(token_index[begin_row:high_key], token_start[begin_row:high_key], token_index[low_key:high_key], token_start[low_key:high_key])
        scores = jnp.einsum("qhgd,khd->hgqk", query_function[begin_row:high_key], key_f[low_key:high_key]) * factor
        return low_key, high_key, allowed[None, None], scores

    attended_parts = []
    log_parts = []
    for begin_row in range(0, token_total_count, span_rows):
        low_key, high_key, allowed, scores = block_scores(begin_row)
        best_score = jnp.max(jnp.where(allowed, scores, neg_large), axis=3)
        weights = jnp.where(allowed, jnp.exp(scores - best_score[..., None]), 0.0)
        mass_sum = jnp.sum(weights, axis=3)
        summed = jnp.einsum("hgqk,khd->qhgd", rounded(weights), value_f[low_key:high_key])
        attended_block = summed / jnp.transpose(mass_sum, (2, 0, 1))[..., None]
        attended_parts.append(attended_block.reshape(span_rows, QUERY_HEADS, HEAD_SIZE).astype(jnp.bfloat16))
        log_parts.append(best_score + jnp.log(mass_sum))
    attended_output = jnp.concatenate(attended_parts, axis=0)
    log_mass = jnp.concatenate(log_parts, axis=2)
    output = jnp.dot(attended_output.reshape(token_total_count, QUERY_HEADS * HEAD_SIZE), w_out, preferred_element_type=jnp.float32).astype(jnp.bfloat16)

    attended_gradient = jnp.dot(grad_out, w_out.T, preferred_element_type=jnp.float32).astype(jnp.bfloat16)
    gradient_function = attended_gradient.astype(jnp.float32).reshape(token_total_count, KEY_VALUE_HEADS, query_groups, HEAD_SIZE)
    delta_totals = jnp.sum(gradient_function * attended_output.astype(jnp.float32).reshape(token_total_count, KEY_VALUE_HEADS, query_groups, HEAD_SIZE), axis=3)
    key_gradient = jnp.zeros((token_total_count, KEY_VALUE_HEADS, HEAD_SIZE), jnp.float32)
    value_gradient = jnp.zeros((token_total_count, KEY_VALUE_HEADS, HEAD_SIZE), jnp.float32)
    query_parts = []
    for begin_row in range(0, token_total_count, span_rows):
        low_key, high_key, allowed, scores = block_scores(begin_row)
        prob = jnp.where(allowed, jnp.exp(scores - log_mass[:, :, begin_row:high_key][..., None]), 0.0)
        dprob = jnp.einsum("qhgd,khd->hgqk", gradient_function[begin_row:high_key], value_f[low_key:high_key])
        dscore = prob * (dprob - jnp.transpose(delta_totals[begin_row:high_key], (1, 2, 0))[..., None])
        dscore_r = rounded(dscore)
        prob_r = rounded(prob)
        grad_q = jnp.einsum("hgqk,khd->qhgd", dscore_r, key_f[low_key:high_key]) * factor
        query_parts.append(inverse_rotation(grad_q.reshape(span_rows, QUERY_HEADS, HEAD_SIZE), cosine_table[begin_row:high_key], sine_table[begin_row:high_key]).astype(jnp.bfloat16))
        key_gradient = key_gradient.at[low_key:high_key].add(jnp.einsum("hgqk,qhgd->khd", dscore_r, query_function[begin_row:high_key]) * factor)
        value_gradient = value_gradient.at[low_key:high_key].add(jnp.einsum("hgqk,qhgd->khd", prob_r, gradient_function[begin_row:high_key]))
    query_back = jnp.concatenate(query_parts, axis=0).reshape(token_total_count, QUERY_HEADS * HEAD_SIZE)
    key_backward = inverse_rotation(key_gradient, cosine_table, sine_table).astype(jnp.bfloat16).reshape(token_total_count, KEY_VALUE_HEADS * HEAD_SIZE)
    value_backward = value_gradient.astype(jnp.bfloat16).reshape(token_total_count, KEY_VALUE_HEADS * HEAD_SIZE)
    grad_sum = jnp.dot(query_back, w_query.T, preferred_element_type=jnp.float32)
    grad_sum = grad_sum + jnp.dot(key_backward, w_key.T, preferred_element_type=jnp.float32)
    grad_sum = grad_sum + jnp.dot(value_backward, value_weight.T, preferred_element_type=jnp.float32)
    return output, grad_sum.astype(jnp.bfloat16)
```

```python
import functools

import jax
import jax.numpy as jnp
from jax import lax
from jax.experimental import pallas as pl
from jax.experimental.pallas import tpu as pltpu
from jax.sharding import PartitionSpec as P

theta_base = 1000000.0
neg_large = -1e30
log2e = 1.4426950408889634
HEAD = 128
F32 = jnp.float32
BF16 = jnp.bfloat16


def start_of(token_index, doc_starts, doc_ends):
    inside = (token_index[:, None] >= doc_starts[None, :]) & (
        token_index[:, None] < doc_ends[None, :]
    )
    return jnp.sum(jnp.where(inside, doc_starts[None, :], 0), axis=1)


def rope_tables(position):
    half = HEAD // 2
    frequency = theta_base ** (-2.0 * jnp.arange(half, dtype=F32) / HEAD)
    angles = position.astype(F32)[:, None] * frequency[None, :]
    cos, sin = jnp.cos(angles), jnp.sin(angles)
    return jnp.concatenate([cos, cos], axis=1), jnp.concatenate([-sin, sin], axis=1)


def swap_halves(u):
    return jnp.concatenate([u[:, HEAD // 2 :], u[:, : HEAD // 2]], axis=1)


def nn(a, b):
    return lax.dot_general(a, b, (((1,), (0,)), ((), ())), preferred_element_type=F32)


def nt(a, b):
    return lax.dot_general(a, b, (((1,), (1,)), ((), ())), preferred_element_type=F32)


def key_mask(block, rows, first_key, row_index):
    key_index = block * rows + lax.broadcasted_iota(jnp.int32, (rows, rows), 0)
    return (key_index >= first_key) & (key_index <= row_index)


def forward_kernel(meta_ref, start_ref, q_ref, kv_ref, o_ref, lse_ref, qt, m_s, l_s, acc):
    groups, rows, _ = q_ref.shape
    mine, low = meta_ref[0], meta_ref[1]
    scale = HEAD**-0.5 * log2e
    first_key = start_ref[...]
    row_index = mine * rows + lax.broadcasted_iota(jnp.int32, (1, rows), 1)
    for h in range(groups):
        qt[h] = q_ref[h].T

    def block_step(block, first):
        k = kv_ref[block, :, :HEAD]
        vt = kv_ref[block, :, HEAD:].T
        allowed = key_mask(block, rows, first_key, row_index)
        for h in range(groups):
            s = jnp.where(allowed, nn(k, qt[h]) * scale, neg_large)
            top = jnp.max(s, axis=0, keepdims=True)
            if not first:
                old = m_s[pl.ds(h, 1), :]
                top = jnp.maximum(old, top)
            p = jnp.exp2(s - top)
            mass = jnp.sum(p, axis=0, keepdims=True)
            part = nn(vt, p.astype(BF16))
            if first:
                acc[h] = part
            else:
                shrink = jnp.exp2(old - top)
                mass = mass + l_s[pl.ds(h, 1), :] * shrink
                acc[h] = acc[h] * shrink + part
            l_s[pl.ds(h, 1), :] = mass
            m_s[pl.ds(h, 1), :] = top

    block_step(mine, True)

    def body(i, _):
        block_step(mine - i, False)
        return 0

    lax.fori_loop(1, mine - low + 1, body, 0)
    for h in range(groups):
        mass = l_s[pl.ds(h, 1), :]
        o_ref[:, h * HEAD : (h + 1) * HEAD] = (acc[h] / mass).T.astype(BF16)
        lse_ref[pl.ds(h, 1), :] = m_s[pl.ds(h, 1), :] + jnp.log2(mass)


def backward_kernel(
    meta_ref, start_ref, q_ref, g_ref, o_ref, lse_ref, kv_ref, cos_ref, sin_ref,
    dq_ref, dkv_ref, qt, gt, delta_s, dqt,
):
    groups, rows, _ = q_ref.shape
    mine, low = meta_ref[0], meta_ref[1]
    factor = HEAD**-0.5
    scale = factor * log2e
    first_key = start_ref[...]
    row_index = mine * rows + lax.broadcasted_iota(jnp.int32, (1, rows), 1)
    for h in range(groups):
        cols = slice(h * HEAD, (h + 1) * HEAD)
        g_t = g_ref[:, cols].astype(F32).T
        o_t = o_ref[:, cols].astype(F32).T
        qt[h] = q_ref[h].T
        gt[h] = g_t.astype(BF16)
        delta_s[pl.ds(h, 1), :] = jnp.sum(g_t * o_t, axis=0, keepdims=True)
        dqt[h] = jnp.zeros_like(dqt[h])

    def zero(b, _):
        dkv_ref[b] = jnp.zeros_like(dkv_ref[b])
        return 0

    lax.fori_loop(0, low, zero, 0)
    lax.fori_loop(mine + 1, dkv_ref.shape[0], zero, 0)

    def body(i, _):
        block = low + i
        k = kv_ref[block, :, :HEAD]
        v = kv_ref[block, :, HEAD:]
        kt = k.T
        allowed = key_mask(block, rows, first_key, row_index)
        dk = jnp.zeros((rows, HEAD), F32)
        dv = jnp.zeros((rows, HEAD), F32)
        for h in range(groups):
            s = nn(k, qt[h]) * scale
            p = jnp.where(allowed, jnp.exp2(s - lse_ref[pl.ds(h, 1), :]), 0.0)
            ds = p * (nn(v, gt[h]) - delta_s[pl.ds(h, 1), :])
            pb, dsb = p.astype(BF16), ds.astype(BF16)
            dv = dv + nn(pb, g_ref[:, h * HEAD : (h + 1) * HEAD])
            dk = dk + nn(dsb, q_ref[h])
            dqt[h] = dqt[h] + nn(kt, dsb)
        dkv_ref[block, :, :HEAD] = (dk * factor).astype(BF16)
        dkv_ref[block, :, HEAD:] = dv.astype(BF16)
        return 0

    lax.fori_loop(0, mine - low + 1, body, 0)
    cos, sin = cos_ref[...], sin_ref[...]
    for h in range(groups):
        u = dqt[h].T * factor
        dq_ref[:, h * HEAD : (h + 1) * HEAD] = (u * cos - swap_halves(u) * sin).astype(BF16)


def vmem():
    return pl.BlockSpec(memory_space=pltpu.VMEM)


def smem():
    return pl.BlockSpec(memory_space=pltpu.SMEM)


def local(
    tokens, w_query, b_query, w_key, key_bias, value_weight, value_bias, w_out, doc_lengths, grad_out
):
    shards = lax.axis_size("seq")
    mine = lax.axis_index("seq")
    rows = tokens.shape[0]
    groups = w_query.shape[1] // HEAD
    doc_ends = jnp.cumsum(doc_lengths)
    doc_starts = doc_ends - doc_lengths
    index = mine * rows + jnp.arange(rows, dtype=jnp.int32)
    start = start_of(index, doc_starts, doc_ends)
    cos, sin = rope_tables(index - start)
    full_tokens = lax.all_gather(tokens, "tp", axis=1, tiled=True)
    full_grads = lax.all_gather(grad_out, "tp", axis=1, tiled=True)

    def rotated(raw, bias):
        u = (raw + bias.astype(F32)).reshape(rows, -1, HEAD)
        swapped = jnp.concatenate([u[..., HEAD // 2 :], u[..., : HEAD // 2]], axis=-1)
        return (u * cos[:, None] + swapped * sin[:, None]).astype(BF16)

    key = rotated(nn(full_tokens, w_key), key_bias)[:, 0]
    value = (nn(full_tokens, value_weight) + value_bias.astype(F32)).astype(BF16)
    query = jnp.transpose(rotated(nn(full_tokens, w_query), b_query), (1, 0, 2))
    pair = jnp.concatenate([key, value], axis=1)
    pairs = lax.all_gather(pair, "seq", axis=0, tiled=False)
    grad_attended = nt(full_grads, w_out).astype(BF16)
    meta = jnp.stack([mine, start[0] // rows]).astype(jnp.int32)
    start_row = start[None, :].astype(jnp.int32)
    stats = jax.ShapeDtypeStruct((8, rows), F32)
    params = pltpu.CompilerParams(vmem_limit_bytes=48 << 20)
    attended, lse = pl.pallas_call(
        forward_kernel,
        out_shape=(jax.ShapeDtypeStruct((rows, groups * HEAD), BF16), stats),
        in_specs=[smem(), vmem(), vmem(), vmem()],
        out_specs=(vmem(), vmem()),
        scratch_shapes=[
            pltpu.VMEM((groups, HEAD, rows), BF16),
            pltpu.VMEM((8, rows), F32),
            pltpu.VMEM((8, rows), F32),
            pltpu.VMEM((groups, HEAD, rows), F32),
        ],
        compiler_params=params,
        name="attention_forward",
    )(meta, start_row, query, pairs)
    output = lax.psum_scatter(
        nn(attended, w_out).astype(BF16), "tp", scatter_dimension=1, tiled=True
    )
    query_back, pair_grads = pl.pallas_call(
        backward_kernel,
        out_shape=(
            jax.ShapeDtypeStruct((rows, groups * HEAD), BF16),
            jax.ShapeDtypeStruct((shards, rows, 2 * HEAD), BF16),
        ),
        in_specs=[smem()] + [vmem()] * 8,
        out_specs=(vmem(), vmem()),
        scratch_shapes=[
            pltpu.VMEM((groups, HEAD, rows), BF16),
            pltpu.VMEM((groups, HEAD, rows), BF16),
            pltpu.VMEM((8, rows), F32),
            pltpu.VMEM((groups, HEAD, rows), F32),
        ],
        compiler_params=params,
        name="attention_backward",
    )(meta, start_row, query, grad_attended, attended, lse, pairs, cos, sin)
    own = lax.psum_scatter(pair_grads, "seq", scatter_dimension=0, tiled=False).astype(F32)
    key_grad = own[:, :HEAD]
    key_back = (key_grad * cos - swap_halves(key_grad) * sin).astype(BF16)
    value_back = own[:, HEAD:].astype(BF16)
    partial = nt(query_back, w_query) + nt(key_back, w_key) + nt(value_back, value_weight)
    grad_tokens = lax.psum_scatter(partial.astype(BF16), "tp", scatter_dimension=1, tiled=True)
    return output, grad_tokens


def solution(mesh):
    return jax.shard_map(
        local,
        mesh=mesh,
        in_specs=(
            P("seq", "tp"),
            P(None, "tp"),
            P("tp"),
            P(None, "tp"),
            P("tp"),
            P(None, "tp"),
            P("tp"),
            P("tp", None),
            P(),
            P("seq", "tp"),
        ),
        out_specs=(P("seq", "tp"), P("seq", "tp")),
        check_vma=False,
    )
```

```python
import functools

import jax
import jax.numpy as jnp
from jax import lax
from jax.experimental import pallas as pl
from jax.experimental.pallas import tpu as pltpu
from jax.sharding import PartitionSpec as P

theta_base = 1000000.0
neg_large = -1e30
log2e = 1.4426950408889634
HEAD = 128
ROWS = 256
HALF = 128
CHUNK = 64
HEADS = 5
WIDTH = 1280
FEAT = HEADS * HEAD
CHIPS = 16
REACH = 8
F32 = jnp.float32
BF16 = jnp.bfloat16
MESH = pl.DeviceIdType.MESH
factor = HEAD**-0.5
scale = factor * log2e


def start_of(token_index, doc_starts, doc_ends):
    inside = (token_index[:, None] >= doc_starts[None, :]) & (
        token_index[:, None] < doc_ends[None, :]
    )
    return jnp.sum(jnp.where(inside, doc_starts[None, :], 0), axis=1)


def rope_tables(position):
    half = HEAD // 2
    frequency = theta_base ** (-2.0 * jnp.arange(half, dtype=F32) / HEAD)
    angles = position.astype(F32)[:, None] * frequency[None, :]
    cos, sin = jnp.cos(angles), jnp.sin(angles)
    return jnp.concatenate([cos, cos], axis=1), jnp.concatenate([-sin, sin], axis=1)


def nn(a, b):
    return lax.dot_general(a, b, (((1,), (0,)), ((), ())), preferred_element_type=F32)


def nt(a, b):
    return lax.dot_general(a, b, (((1,), (1,)), ((), ())), preferred_element_type=F32)


def block_kernel(
    tok, grad, wq_hbm, wk_hbm, wv_hbm, wo_hbm, bias, cos_ref, sin_ref, start_ref,
    out_ref, gtok_ref,
    w, wo, tk, gr, acc, gacc, qn, qt, gn, gt, kv, at, att, oacc, m_s, l_s, lse, delta,
    tmp, own, sib_out, sib_in, dkv_out, dkv_in, x, p_out, v_out, f_out, p_grad, v_grad, f_grad,
    wsem, ys, yr, fs, fr, kvs, kvr, sbs, sbr, dss, dsr, dos, dor, rss, rsr,
):
    s = lax.axis_index("seq")
    t = lax.axis_index("tp")
    chip, core = lax.div(s, 2), lax.rem(s, 2)
    right, left, opp = lax.rem(t + 1, 4), lax.rem(t + 3, 4), lax.rem(t + 2, 4)
    to_right, to_left = {"seq": s, "tp": right}, {"seq": s, "tp": left}
    sibling = {"seq": s + 1 - 2 * core, "tp": t}

    def remote(src, dst, send, recv, device):
        return pltpu.make_async_remote_copy(
            src_ref=src, dst_ref=dst, send_sem=send, recv_sem=recv,
            device_id=device, device_id_type=MESH,
        )

    loads = []
    for i in range(4):
        for j, (ref, lo, hi) in enumerate(
            ((wq_hbm, 0, FEAT), (wk_hbm, FEAT, FEAT + HEAD), (wv_hbm, FEAT + HEAD, FEAT + 2 * HEAD))
        ):
            loads.append(
                pltpu.make_async_copy(
                    ref.at[pl.ds(i * WIDTH, WIDTH)], w.at[i, :, lo:hi], wsem.at[3 * i + j]
                )
            )
    loads_out = [
        pltpu.make_async_copy(wo_hbm.at[:, pl.ds(i * WIDTH, WIDTH)], wo.at[i], wsem.at[12 + i])
        for i in range(4)
    ]
    for copy in loads + loads_out:
        copy.start()

    barrier = pltpu.get_barrier_semaphore()
    for device in (to_right, to_left, sibling):
        pl.semaphore_signal(barrier, inc=1, device_id=device, device_id_type=MESH)
    for d in range(1, REACH + 1):
        @pl.when(chip + d < CHIPS)
        def _():
            pl.semaphore_signal(
                barrier, inc=1, device_id={"seq": s + 2 * d, "tp": t}, device_id_type=MESH
            )

        @pl.when(chip >= d)
        def _():
            pl.semaphore_signal(
                barrier, inc=1, device_id={"seq": s - 2 * d, "tp": t}, device_id_type=MESH
            )
    pl.semaphore_wait(
        barrier, 3 + jnp.minimum(chip, REACH) + jnp.minimum(CHIPS - 1 - chip, REACH)
    )

    def unit(u):
        src, buf = (tok, tk) if u < 4 else (grad, gr)
        return src, buf, pl.ds((u % 4) * CHUNK, CHUNK)

    def send(u, way):
        src, buf, sl = unit(u)
        if way == 0:
            return remote(src.at[sl], buf.at[0, sl], ys.at[u, 0], yr.at[u, 0], to_right)
        return remote(src.at[sl], buf.at[2, sl], ys.at[u, 1], yr.at[u, 1], to_left)

    def forward(u):
        _, buf, sl = unit(u)
        if u % 2 == 0:
            return remote(buf.at[0, sl], buf.at[1, sl], fs.at[u], fr.at[u], to_right)
        return remote(buf.at[2, sl], buf.at[1, sl], fs.at[u], fr.at[u], to_left)

    def issue(u):
        for way in range(2):
            send(u, way).start()

    def pump(u):
        send(u, u % 2).wait_recv()
        forward(u).start()

    def rest(u):
        send(u, 1 - u % 2).wait_recv()

    def kv_send(d, hf):
        here = kv.at[chip, core, hf]
        return remote(here, here, kvs.at[d - 1, hf], kvr.at[d - 1, hf], {"seq": s + 2 * d, "tp": t})

    def kv_arrival(d, hf):
        there = kv.at[chip - d, core, hf]
        return remote(there, there, kvs.at[d - 1, hf], kvr.at[d - 1, hf], sibling)

    def kv_sibling(d, hf):
        there = kv.at[chip - d, core, hf]
        return remote(there, there, sbs.at[d, hf], sbr.at[d, hf], sibling)

    def make_rows(hf):
        sl = pl.ds(hf * HALF, HALF)
        cos, sin = cos_ref[sl, :], sin_ref[sl, :]

        def rotated(i):
            u = acc[sl, i * HEAD : (i + 1) * HEAD] + bias[:, i * HEAD : (i + 1) * HEAD]
            return (u * cos + pltpu.roll(u, HEAD // 2, 1) * sin).astype(BF16)

        kv[chip, core, hf, :, :HEAD] = rotated(HEADS)
        kv[chip, core, hf, :, HEAD:] = (
            acc[sl, (HEADS + 1) * HEAD :] + bias[:, (HEADS + 1) * HEAD :]
        ).astype(BF16)
        kv_sibling(0, hf).start()
        for d in range(1, REACH + 1):
            @pl.when(chip + d < CHIPS)
            def _():
                kv_send(d, hf).start()
        for h in range(HEADS):
            q = rotated(h)
            qn[h, sl, :] = q
            qt[:, pl.ds(h * ROWS + hf * HALF, HALF)] = q.T

    issue(0)
    issue(1)
    for copy in loads:
        copy.wait()
    acc[...] = nn(tok[...], w[t])
    pump(0)
    issue(2)
    for copy in loads_out:
        copy.wait()
    gacc[...] = nt(grad[...], wo[t])
    m_s[...] = jnp.full(m_s.shape, neg_large, F32)
    l_s[...] = jnp.zeros(l_s.shape, F32)
    oacc[...] = jnp.zeros(oacc.shape, F32)
    pump(1)
    issue(3)
    for hf in range(2):
        sl = pl.ds(hf * HALF, HALF)
        if hf == 1:
            pump(2)
            issue(4)
            pump(3)
            issue(5)
        for u in (2 * hf, 2 * hf + 1):
            rest(u)
        acc[sl, :] += nn(tk[0, sl, :], w[left])
        acc[sl, :] += nn(tk[2, sl, :], w[right])
        for u in (2 * hf, 2 * hf + 1):
            forward(u).wait_recv()
        acc[sl, :] += nn(tk[1, sl, :], w[opp])
        make_rows(hf)

    for hf in range(2):
        for d in range(1, REACH + 1):
            @pl.when(chip >= d)
            def _():
                kv_arrival(d, hf).wait_recv()
                kv_sibling(d, hf).start()

    first_key = start_ref[...]
    row_index = s * ROWS + lax.broadcasted_iota(jnp.int32, (1, ROWS), 1)

    def attend(d):
        both = kv[chip - d].reshape(4 * HALF, 2 * HEAD)
        k = both[:, :HEAD]
        vt = both[:, HEAD:].T
        key = (chip - d) * (4 * HALF) + lax.broadcasted_iota(jnp.int32, (4 * HALF, ROWS), 0)
        allowed = (key >= first_key) & (key <= row_index)
        following = nn(k, qt[:, :ROWS])
        held = None
        for h in range(HEADS + 1):
            sl = slice(h * ROWS, (h + 1) * ROWS)
            raw = following
            if h + 1 < HEADS:
                following = nn(k, qt[:, (h + 1) * ROWS : (h + 2) * ROWS])
            if held is not None:
                cols, weights, shrink = held
                oacc[:, cols] = oacc[:, cols] * shrink + nn(vt, weights)
            if h < HEADS:
                scores = jnp.where(allowed, raw * scale, neg_large)
                old = m_s[:, sl]
                top = jnp.maximum(old, jnp.max(scores, axis=0, keepdims=True))
                weights = jnp.exp2(scores - top)
                shrink = jnp.exp2(old - top)
                l_s[:, sl] = l_s[:, sl] * shrink + jnp.sum(weights, axis=0, keepdims=True)
                m_s[:, sl] = top
                held = (sl, weights.astype(BF16), shrink)

    pump(4)
    issue(6)

    def forward_step(d, carry):
        @pl.when(chip >= d)
        def _():
            for hf in range(2):
                kv_sibling(d, hf).wait_recv()
            attend(d)

        @pl.when(d == 2)
        def _():
            pump(5)
            issue(7)

        @pl.when(d == 6)
        def _():
            pump(6)

        return carry

    lax.fori_loop(0, REACH + 1, forward_step, 0)
    for h in range(HEADS):
        sl = slice(h * ROWS, (h + 1) * ROWS)
        mass = l_s[:, sl]
        o = (oacc[:, sl] / mass).astype(BF16)
        att[:, sl] = o
        at[:, h * HEAD : (h + 1) * HEAD] = o.T
        lse[:, sl] = m_s[:, sl] + jnp.log2(mass)

    def scatter_copy(i, part, arrived, passing, n):
        a, b = pl.ds(0, HALF), pl.ds(HALF, HALF)
        src, dst, device = (
            (part.at[1, a], passing.at[0], to_right),
            (part.at[1, b], passing.at[1], to_left),
            (part.at[2, b], arrived.at[0, b], to_right),
            (part.at[0, a], arrived.at[1, a], to_left),
            (part.at[2, a], arrived.at[0, a], to_right),
            (part.at[0, b], arrived.at[1, b], to_left),
        )[i]
        return remote(src, dst, rss.at[n, i], rsr.at[n, i], device)

    def scatter_early(share, part, arrived, passing, n):
        for i, (slot, rel, hf) in enumerate(((opp, 1, 0), (opp, 1, 1), (right, 2, 1), (left, 0, 0))):
            part[rel, pl.ds(hf * HALF, HALF), :] = share(slot, hf).astype(BF16)
            scatter_copy(i, part, arrived, passing, n).start()

    def scatter_late(share, part, arrived, passing, n):
        for i, (slot, rel, hf) in enumerate(((right, 2, 0), (left, 0, 1))):
            mine = share(slot, hf)
            scatter_copy(i, part, arrived, passing, n).wait_recv()
            part[rel, pl.ds(hf * HALF, HALF), :] = (mine + passing[i].astype(F32)).astype(BF16)
            scatter_copy(4 + i, part, arrived, passing, n).start()

    def scatter_end(share, part, arrived, passing, n, result):
        for hf, waits in ((1, (2, 5)), (0, (3, 4))):
            sl = pl.ds(hf * HALF, HALF)
            mine = share(t, hf)
            for i in waits:
                scatter_copy(i, part, arrived, passing, n).wait_recv()
            result[sl, :] = (
                mine + arrived[0, sl, :].astype(F32) + arrived[1, sl, :].astype(F32)
            ).astype(BF16)
        for i in range(6):
            scatter_copy(i, part, arrived, passing, n).wait_send()

    def out_share(slot, hf):
        return nn(at[pl.ds(hf * HALF, HALF), :], wo[slot])

    pump(7)
    scatter_early(out_share, p_out, v_out, f_out, 0)

    for hf in range(2):
        sl = pl.ds(hf * HALF, HALF)
        for u in (4 + 2 * hf, 5 + 2 * hf):
            rest(u)
            forward(u).wait_recv()
        g = gacc[sl, :] + nt(gr[0, sl, :], wo[left])
        g = g + nt(gr[2, sl, :], wo[right])
        g = (g + nt(gr[1, sl, :], wo[opp])).astype(BF16)
        for h in range(HEADS):
            part = g[:, h * HEAD : (h + 1) * HEAD]
            gn[h, sl, :] = part
            gt[:, pl.ds(h * ROWS + hf * HALF, HALF)] = part.T
    delta[...] = jnp.sum(gt[...].astype(F32) * att[...].astype(F32), axis=0, keepdims=True)
    oacc[...] = jnp.zeros(oacc.shape, F32)

    def dkv_sibling(d, hf):
        return remote(sib_out.at[d, hf], sib_in.at[d, hf], dss.at[d, hf], dsr.at[d, hf], sibling)

    def dkv_send(d, hf):
        return remote(
            dkv_out.at[d - 1, hf], dkv_in.at[d - 1, hf], dos.at[d - 1, hf], dor.at[d - 1, hf],
            {"seq": s - 2 * d, "tp": t},
        )

    def backward(d, hf):
        both = kv[chip - d, :, hf].reshape(2 * HALF, 2 * HEAD)
        k, v = both[:, :HEAD], both[:, HEAD:]
        kt = k.T
        r = lax.broadcasted_iota(jnp.int32, (2 * HALF, ROWS), 0)
        key = (chip - d) * (4 * HALF) + hf * HALF + jnp.where(r >= HALF, r + HALF, r)
        allowed = (key >= first_key) & (key <= row_index)
        following = (nn(k, qt[:, :ROWS]), nn(v, gt[:, :ROWS]))
        held = None
        dk = jnp.zeros((2 * HALF, HEAD), F32)
        dv = jnp.zeros((2 * HALF, HEAD), F32)
        for h in range(HEADS + 1):
            sl = slice(h * ROWS, (h + 1) * ROWS)
            raw, dprob = following
            if h + 1 < HEADS:
                nxt = slice((h + 1) * ROWS, (h + 2) * ROWS)
                following = (nn(k, qt[:, nxt]), nn(v, gt[:, nxt]))
            if held is not None:
                cols, prob_b, ds_b = held
                dv = dv + nn(prob_b, gn[h - 1])
                dk = dk + nn(ds_b, qn[h - 1])
                oacc[:, cols] = oacc[:, cols] + nn(kt, ds_b)
            if h < HEADS:
                prob = jnp.where(allowed, jnp.exp2(raw * scale - lse[:, sl]), 0.0)
                ds = prob * (dprob - delta[:, sl])
                held = (sl, prob.astype(BF16), ds.astype(BF16))
        tmp[:, :, :HEAD] = (dk * factor).reshape(2, HALF, HEAD)
        tmp[:, :, HEAD:] = dv.reshape(2, HALF, HEAD)
        own[d, hf] = tmp[core]
        sib_out[d, hf] = tmp[1 - core].astype(BF16)
        dkv_sibling(d, hf).start()

    def dkv_pump(i):
        d, hf = REACH - lax.div(i, 2), lax.rem(i, 2)

        @pl.when((chip >= d) & (d > 0))
        def _():
            dkv_sibling(d, hf).wait_recv()
            dkv_out[d - 1, hf] = (own[d, hf] + sib_in[d, hf].astype(F32)).astype(BF16)
            dkv_send(d, hf).start()

    def backward_step(i, carry):
        d, hf = REACH - lax.div(i, 2), lax.rem(i, 2)

        @pl.when(chip >= d)
        def _():
            backward(d, hf)

        @pl.when(i > 0)
        def _():
            dkv_pump(i - 1)

        @pl.when(i == 10)
        def _():
            scatter_late(out_share, p_out, v_out, f_out, 0)

        return carry

    lax.fori_loop(0, 2 * (REACH + 1), backward_step, 0)
    for h in range(HEADS):
        u = oacc[:, h * ROWS : (h + 1) * ROWS].T * factor
        x[:, h * HEAD : (h + 1) * HEAD] = (
            u * cos_ref[...] - pltpu.roll(u, HEAD // 2, 1) * sin_ref[...]
        ).astype(BF16)
    for hf in range(2):
        dkv_sibling(0, hf).wait_recv()
        own[0, hf] = own[0, hf] + sib_in[0, hf].astype(F32)
        for d in range(1, REACH + 1):
            @pl.when(chip + d < CHIPS)
            def _():
                dkv_send(d, hf).wait_recv()
                own[0, hf] = own[0, hf] + dkv_in[d - 1, hf].astype(F32)
        sl = pl.ds(hf * HALF, HALF)
        u = own[0, hf, :, :HEAD]
        x[sl, FEAT : FEAT + HEAD] = (
            u * cos_ref[sl, :] - pltpu.roll(u, HEAD // 2, 1) * sin_ref[sl, :]
        ).astype(BF16)
        x[sl, FEAT + HEAD :] = own[0, hf, :, HEAD:].astype(BF16)

    def grad_share(slot, hf):
        return nt(x[pl.ds(hf * HALF, HALF), :], w[slot])

    scatter_early(grad_share, p_grad, v_grad, f_grad, 1)
    scatter_end(out_share, p_out, v_out, f_out, 0, out_ref)
    scatter_late(grad_share, p_grad, v_grad, f_grad, 1)

    for u in range(8):
        for way in range(2):
            send(u, way).wait_send()
        forward(u).wait_send()
    for hf in range(2):
        kv_sibling(0, hf).wait_send()
        dkv_sibling(0, hf).wait_send()
        for d in range(1, REACH + 1):
            @pl.when(chip + d < CHIPS)
            def _():
                kv_send(d, hf).wait_send()

            @pl.when(chip >= d)
            def _():
                kv_sibling(d, hf).wait_send()
                dkv_sibling(d, hf).wait_send()
                dkv_send(d, hf).wait_send()
    scatter_end(grad_share, p_grad, v_grad, f_grad, 1, gtok_ref)


def local(
    tokens, w_query, b_query, w_key, key_bias, value_weight, value_bias, w_out, doc_lengths, grad_out
):
    mine = lax.axis_index("seq")
    doc_ends = jnp.cumsum(doc_lengths)
    doc_starts = doc_ends - doc_lengths
    index = mine * ROWS + jnp.arange(ROWS, dtype=jnp.int32)
    start = start_of(index, doc_starts, doc_ends)
    cos, sin = rope_tables(index - start)
    bias = jnp.concatenate([b_query, key_bias, value_bias]).astype(F32)[None, :]
    vm = pl.BlockSpec(memory_space=pltpu.VMEM)
    hbm = pl.BlockSpec(memory_space=pl.ANY)
    dma = pltpu.SemaphoreType.DMA
    shape = jax.ShapeDtypeStruct((ROWS, WIDTH), BF16)
    return pl.pallas_call(
        block_kernel,
        out_shape=(shape, shape),
        in_specs=[vm, vm, hbm, hbm, hbm, hbm, vm, vm, vm, vm],
        out_specs=(vm, vm),
        scratch_shapes=[
            pltpu.VMEM((4, WIDTH, FEAT + 2 * HEAD), BF16),
            pltpu.VMEM((4, FEAT, WIDTH), BF16),
            pltpu.VMEM((3, ROWS, WIDTH), BF16),
            pltpu.VMEM((3, ROWS, WIDTH), BF16),
            pltpu.VMEM((ROWS, FEAT + 2 * HEAD), F32),
            pltpu.VMEM((ROWS, FEAT), F32),
            pltpu.VMEM((HEADS, ROWS, HEAD), BF16),
            pltpu.VMEM((HEAD, HEADS * ROWS), BF16),
            pltpu.VMEM((HEADS, ROWS, HEAD), BF16),
            pltpu.VMEM((HEAD, HEADS * ROWS), BF16),
            pltpu.VMEM((CHIPS, 2, 2, HALF, 2 * HEAD), BF16),
            pltpu.VMEM((ROWS, FEAT), BF16),
            pltpu.VMEM((HEAD, HEADS * ROWS), BF16),
            pltpu.VMEM((HEAD, HEADS * ROWS), F32),
            pltpu.VMEM((1, HEADS * ROWS), F32),
            pltpu.VMEM((1, HEADS * ROWS), F32),
            pltpu.VMEM((1, HEADS * ROWS), F32),
            pltpu.VMEM((1, HEADS * ROWS), F32),
            pltpu.VMEM((2, HALF, 2 * HEAD), F32),
            pltpu.VMEM((REACH + 1, 2, HALF, 2 * HEAD), F32),
            pltpu.VMEM((REACH + 1, 2, HALF, 2 * HEAD), BF16),
            pltpu.VMEM((REACH + 1, 2, HALF, 2 * HEAD), BF16),
            pltpu.VMEM((REACH, 2, HALF, 2 * HEAD), BF16),
            pltpu.VMEM((REACH, 2, HALF, 2 * HEAD), BF16),
            pltpu.VMEM((ROWS, FEAT + 2 * HEAD), BF16),
            pltpu.VMEM((3, ROWS, WIDTH), BF16),
            pltpu.VMEM((2, ROWS, WIDTH), BF16),
            pltpu.VMEM((2, HALF, WIDTH), BF16),
            pltpu.VMEM((3, ROWS, WIDTH), BF16),
            pltpu.VMEM((2, ROWS, WIDTH), BF16),
            pltpu.VMEM((2, HALF, WIDTH), BF16),
            dma((16,)),
            dma((8, 2)), dma((8, 2)),
            dma((8,)), dma((8,)),
            dma((REACH, 2)), dma((REACH, 2)),
            dma((REACH + 1, 2)), dma((REACH + 1, 2)),
            dma((REACH + 1, 2)), dma((REACH + 1, 2)),
            dma((REACH, 2)), dma((REACH, 2)),
            dma((2, 6)), dma((2, 6)),
        ],
        compiler_params=pltpu.CompilerParams(
            collective_id=0, has_side_effects=True, vmem_limit_bytes=60 << 20
        ),
        name="attention_block",
    )(
        tokens, grad_out, w_query, w_key, value_weight, w_out, bias, cos, sin,
        start[None, :].astype(jnp.int32),
    )


def solution(mesh):
    return jax.shard_map(
        local,
        mesh=mesh,
        in_specs=(
            P("seq", "tp"),
            P(None, "tp"),
            P("tp"),
            P(None, "tp"),
            P("tp"),
            P(None, "tp"),
            P("tp"),
            P("tp", None),
            P(),
            P("seq", "tp"),
        ),
        out_specs=(P("seq", "tp"), P("seq", "tp")),
        check_vma=False,
    )
```

```python
import functools

import jax
import jax.numpy as jnp
import numpy as np
from jax import lax
from jax.experimental import pallas as pl
from jax.experimental.pallas import tpu as pltpu
from jax.sharding import PartitionSpec as P

theta_base = 1000000.0
neg_large = -1e30
log2e = 1.4426950408889634
HEAD = 128
ROWS = 256
HALF = 128
CHUNK = 64
HEADS = 5
WIDTH = 1280
FEAT = HEADS * HEAD
CHIPS = 16
REACH = 8
F32 = jnp.float32
BF16 = jnp.bfloat16
MESH = pl.DeviceIdType.MESH
factor = HEAD**-0.5
scale = factor * log2e


def nn(a, b):
    return lax.dot_general(a, b, (((1,), (0,)), ((), ())), preferred_element_type=F32)


def nt(a, b):
    return lax.dot_general(a, b, (((1,), (1,)), ((), ())), preferred_element_type=F32)


def block_kernel(
    lengths, tok, grad, wq_hbm, wk_hbm, wv_hbm, wo_hbm, bq, bk, bv, freq_ref,
    out_ref, gtok_ref,
    cos_ref, sin_ref, w, wo, tk, gr, acc, gacc, qn, qt, gn, gt, kv, at, att, oacc, m_s, l_s, lse, delta,
    tmp, own, sib_out, sib_in, dkv_out, dkv_in, x, p_out, v_out, f_out, p_grad, v_grad, f_grad,
    wsem, ys, yr, fs, fr, kvs, kvr, sbs, sbr, dss, dsr, dos, dor, rss, rsr,
):
    s = lax.axis_index("seq")
    t = lax.axis_index("tp")
    chip, core = lax.div(s, 2), lax.rem(s, 2)
    right, left, opp = lax.rem(t + 1, 4), lax.rem(t + 3, 4), lax.rem(t + 2, 4)
    to_right, to_left = {"seq": s, "tp": right}, {"seq": s, "tp": left}
    sibling = {"seq": s + 1 - 2 * core, "tp": t}
    at_z, at_x = lax.div(chip, 4), lax.rem(chip, 4)
    m1 = at_x + core * (at_z - at_x)
    m2 = at_z + core * (at_x - at_z)
    stride1, stride2 = 1 + 3 * core, 4 - 3 * core

    def place(r2, r1):
        return lax.rem(m1 + 4 - r1, 4) * stride1 + lax.rem(m2 + 4 - r2, 4) * stride2

    def towards(step2, step1):
        return {"seq": 2 * place(-step2, -step1) + core, "tp": t}

    up1, down1, up2, down2 = towards(0, 1), towards(0, -1), towards(1, 0), towards(-1, 0)

    def remote(src, dst, send, recv, device):
        return pltpu.make_async_remote_copy(
            src_ref=src, dst_ref=dst, send_sem=send, recv_sem=recv,
            device_id=device, device_id_type=MESH,
        )

    loads = []
    for i in range(4):
        for j, (ref, lo, hi) in enumerate(
            ((wq_hbm, 0, FEAT), (wk_hbm, FEAT, FEAT + HEAD), (wv_hbm, FEAT + HEAD, FEAT + 2 * HEAD))
        ):
            loads.append(
                pltpu.make_async_copy(
                    ref.at[pl.ds(i * WIDTH, WIDTH)], w.at[i, :, lo:hi], wsem.at[3 * i + j]
                )
            )
    loads_out = [
        pltpu.make_async_copy(wo_hbm.at[:, pl.ds(i * WIDTH, WIDTH)], wo.at[i], wsem.at[12 + i])
        for i in range(4)
    ]
    for copy in loads + loads_out:
        copy.start()

    barrier = pltpu.get_barrier_semaphore()
    partners = (to_right, to_left, sibling, up1, down1, up2, down2)
    for device in partners:
        pl.semaphore_signal(barrier, inc=1, device_id=device, device_id_type=MESH)
    for d in range(1, REACH + 1):
        @pl.when(chip + d < CHIPS)
        def _():
            pl.semaphore_signal(
                barrier, inc=1, device_id={"seq": s + 2 * d, "tp": t}, device_id_type=MESH
            )

        @pl.when(chip >= d)
        def _():
            pl.semaphore_signal(
                barrier, inc=1, device_id={"seq": s - 2 * d, "tp": t}, device_id_type=MESH
            )
    pl.semaphore_wait(
        barrier,
        len(partners) + jnp.minimum(chip, REACH) + jnp.minimum(CHIPS - 1 - chip, REACH),
    )

    def unit(u):
        src, buf = (tok, tk) if u < 4 else (grad, gr)
        return src, buf, pl.ds((u % 4) * CHUNK, CHUNK)

    def send(u, way):
        src, buf, sl = unit(u)
        if way == 0:
            return remote(src.at[sl], buf.at[0, sl], ys.at[u, 0], yr.at[u, 0], to_right)
        return remote(src.at[sl], buf.at[2, sl], ys.at[u, 1], yr.at[u, 1], to_left)

    def forward(u):
        _, buf, sl = unit(u)
        if u % 2 == 0:
            return remote(buf.at[0, sl], buf.at[1, sl], fs.at[u], fr.at[u], to_right)
        return remote(buf.at[2, sl], buf.at[1, sl], fs.at[u], fr.at[u], to_left)

    def issue(u):
        for way in range(2):
            send(u, way).start()

    def pump(u):
        send(u, u % 2).wait_recv()
        forward(u).start()

    def rest(u):
        send(u, 1 - u % 2).wait_recv()

    def kv_copy(hf, r2, r1):
        if r2 == 0:
            src = (0, 0) if r1 != 2 else (0, 1 + 2 * hf)
            device = up1 if r1 == 1 or (r1 == 2 and hf == 0) else down1
        elif r2 == 2:
            src, device = ((1, r1), up2) if r1 < 2 else ((3, r1), down2)
        else:
            src, device = (0, r1), up2 if r2 == 1 else down2
        here = kv.at[place(*src), core, hf]
        return remote(here, here, kvs.at[hf, r2, r1], kvr.at[hf, r2, r1], device)

    def kv_start(hf, *slots):
        for slot in slots:
            kv_copy(hf, *slot).start()

    def kv_wait(hf, *slots):
        for r2, r1 in slots:
            there = kv.at[place(r2, r1), core, hf]
            remote(there, there, kvs.at[hf, r2, r1], kvr.at[hf, r2, r1], sibling).wait_recv()

    def kv_second(hf):
        kv_wait(hf, (0, 1))
        kv_start(hf, *(((0, 2),) if hf == 0 else ()), (1, 1), (3, 1))
        kv_wait(hf, (0, 3))
        kv_start(hf, *(((0, 2),) if hf == 1 else ()), (1, 3), (3, 3))
        kv_wait(hf, (1, 0))
        kv_start(hf, (2, 0))

    def kv_third(hf):
        kv_wait(hf, (0, 2))
        kv_start(hf, (1, 2), (3, 2))
        kv_wait(hf, (1, 1))
        kv_start(hf, (2, 1))

    def kv_fourth(hf):
        kv_wait(hf, (3, 3))
        kv_start(hf, (2, 3))
        kv_wait(hf, (3, 2))
        kv_start(hf, (2, 2))

    def kv_fifth(hf):
        kv_wait(hf, (1, 2), (1, 3), (3, 0), (3, 1), (2, 0), (2, 1), (2, 2), (2, 3))
        for d in range(1, REACH + 1):
            @pl.when(chip >= d)
            def _():
                kv_sibling(d, hf).start()

    def kv_sibling(d, hf):
        there = kv.at[chip - d, core, hf]
        return remote(there, there, sbs.at[d, hf], sbr.at[d, hf], sibling)

    def make_rows(hf):
        sl = pl.ds(hf * HALF, HALF)
        cos, sin = cos_ref[sl, :], sin_ref[sl, :]

        def rotated(i):
            u = acc[sl, i * HEAD : (i + 1) * HEAD]
            u = u + (bq[:, i * HEAD : (i + 1) * HEAD] if i < HEADS else bk[...]).astype(F32)
            return (u * cos + pltpu.roll(u, HEAD // 2, 1) * sin).astype(BF16)

        kv[chip, core, hf, :, :HEAD] = rotated(HEADS)
        kv[chip, core, hf, :, HEAD:] = (
            acc[sl, (HEADS + 1) * HEAD :] + bv[...].astype(F32)
        ).astype(BF16)
        kv_start(hf, (0, 1), (0, 3), (1, 0), (3, 0))
        kv_sibling(0, hf).start()
        for h in range(HEADS):
            q = rotated(h)
            qn[h, sl, :] = q
            qt[:, pl.ds(h * ROWS + hf * HALF, HALF)] = q.T

    issue(0)
    issue(1)
    end0 = lengths[0]
    end1 = end0 + lengths[1]
    end2 = end1 + lengths[2]

    def start_at(index):
        later = jnp.where(index >= end2, end2, jnp.where(index >= end1, end1, end0))
        return jnp.where(index >= end0, later, 0)

    row_index = s * ROWS + lax.broadcasted_iota(jnp.int32, (1, ROWS), 1)
    first_key = start_at(row_index)
    index = s * ROWS + lax.broadcasted_iota(jnp.int32, (ROWS, HEAD), 0)
    angles = (index - start_at(index)).astype(F32) * freq_ref[...]
    cos_ref[...] = jnp.cos(angles)
    sine = jnp.sin(angles)
    lane = lax.broadcasted_iota(jnp.int32, (ROWS, HEAD), 1)
    sin_ref[...] = jnp.where(lane < HEAD // 2, -sine, sine)

    for copy in loads:
        copy.wait()
    acc[...] = nn(tok[...], w[t])
    pump(0)
    issue(2)
    for copy in loads_out:
        copy.wait()
    gacc[...] = nt(grad[...], wo[t])
    m_s[...] = jnp.full(m_s.shape, neg_large, F32)
    l_s[...] = jnp.zeros(l_s.shape, F32)
    oacc[...] = jnp.zeros(oacc.shape, F32)
    pump(1)
    issue(3)
    for hf in range(2):
        sl = pl.ds(hf * HALF, HALF)
        if hf == 1:
            pump(2)
            issue(4)
            pump(3)
            issue(5)
        for u in (2 * hf, 2 * hf + 1):
            rest(u)
        acc[sl, :] += nn(tk[0, sl, :], w[left])
        acc[sl, :] += nn(tk[2, sl, :], w[right])
        if hf == 1:
            kv_second(0)
        for u in (2 * hf, 2 * hf + 1):
            forward(u).wait_recv()
        acc[sl, :] += nn(tk[1, sl, :], w[opp])
        make_rows(hf)

    r2 = lax.broadcasted_iota(jnp.int32, (2 * HALF, ROWS), 0)
    key_at = jnp.where(r2 >= HALF, r2 + HALF, r2)

    def attend(first, second):
        both = jnp.concatenate(
            [kv[jnp.maximum(c, 0), :, hf].reshape(2 * HALF, 2 * HEAD) for c, hf in (first, second)],
            axis=0,
        )
        k = both[:, :HEAD]
        vt = both[:, HEAD:].T
        key = jnp.concatenate(
            [key_at + (c * (4 * HALF) + hf * HALF) for c, hf in (first, second)], axis=0
        )
        allowed = (key >= first_key) & (key <= row_index)
        following = nn(k, qt[:, :ROWS])
        held = None
        for h in range(HEADS + 1):
            sl = slice(h * ROWS, (h + 1) * ROWS)
            raw = following
            if h + 1 < HEADS:
                following = nn(k, qt[:, (h + 1) * ROWS : (h + 2) * ROWS])
            if held is not None:
                cols, weights, shrink = held
                oacc[:, cols] = oacc[:, cols] * shrink + nn(vt, weights)
            if h < HEADS:
                scores = jnp.where(allowed, raw * scale, neg_large)
                old = m_s[:, sl]
                top = jnp.maximum(old, jnp.max(scores, axis=0, keepdims=True))
                weights = jnp.exp2(scores - top)
                shrink = jnp.exp2(old - top)
                l_s[:, sl] = l_s[:, sl] * shrink + jnp.sum(weights, axis=0, keepdims=True)
                m_s[:, sl] = top
                held = (sl, weights.astype(BF16), shrink)

    def forward_step(i, carry):
        j, hf = lax.rem(i + 3, 4), lax.div(i + 3, 4) - 1
        d = 2 * j + 1
        is_own = i == 0

        @pl.when(i == 1)
        def _():
            kv_third(1)
            pump(4)
            kv_fourth(1)
            kv_fifth(0)

        @pl.when(i == 3)
        def _():
            pump(5)
            kv_fifth(1)

        @pl.when(i == 5)
        def _():
            pump(6)
            pump(7)

        for e in range(2):
            @pl.when((i > 0) & (chip >= d + e))
            def _():
                kv_sibling(d + e, hf).wait_recv()

        @pl.when(is_own | (chip >= d))
        def _():
            attend(
                (jnp.where(is_own, chip, chip - d), jnp.where(is_own, 0, hf)),
                (jnp.where(is_own, chip, chip - d - 1), jnp.where(is_own, 1, hf)),
            )

        return carry

    issue(6)
    issue(7)
    kv_third(0)
    kv_fourth(0)
    kv_second(1)
    for hf in range(2):
        kv_sibling(0, hf).wait_recv()
    lax.fori_loop(0, REACH + 1, forward_step, 0)
    for u in range(4, 8):
        rest(u)
    gacc[...] += nt(gr[0], wo[left])
    gacc[...] += nt(gr[2], wo[right])
    for h in range(HEADS):
        sl = slice(h * ROWS, (h + 1) * ROWS)
        mass = l_s[:, sl]
        o = (oacc[:, sl] / mass).astype(BF16)
        att[:, sl] = o
        at[:, h * HEAD : (h + 1) * HEAD] = o.T
        lse[:, sl] = m_s[:, sl] + jnp.log2(mass)

    def pieces(n):
        return ((0, HALF), (HALF, HALF)) if n == 0 else (
            ((n - 1) * HALF, CHUNK), ((n - 1) * HALF + CHUNK, CHUNK)
        )

    def passing_rows(n):
        return pl.ds(0, HALF) if n == 0 else pl.ds((n - 1) * CHUNK, CHUNK)

    def scatter_copy(i, part, arrived, passing, n):
        a, b = [pl.ds(*piece) for piece in pieces(n)]
        over = passing_rows(n)
        src, dst, device = (
            (part.at[1, a], passing.at[0, over], to_right),
            (part.at[1, b], passing.at[1, over], to_left),
            (part.at[2, b], arrived.at[0, b], to_right),
            (part.at[0, a], arrived.at[1, a], to_left),
            (part.at[2, a], arrived.at[0, a], to_right),
            (part.at[0, b], arrived.at[1, b], to_left),
        )[i]
        return remote(src, dst, rss.at[n, i], rsr.at[n, i], device)

    def scatter_early(share, part, arrived, passing, n):
        for i, (slot, rel, e) in enumerate(((opp, 1, 0), (opp, 1, 1), (right, 2, 1), (left, 0, 0))):
            sl = pl.ds(*pieces(n)[e])
            part[rel, sl, :] = share(slot, sl).astype(BF16)
            scatter_copy(i, part, arrived, passing, n).start()

    def scatter_late(share, part, arrived, passing, n):
        for i, (slot, rel, e) in enumerate(((right, 2, 0), (left, 0, 1))):
            sl = pl.ds(*pieces(n)[e])
            mine = share(slot, sl)
            scatter_copy(i, part, arrived, passing, n).wait_recv()
            part[rel, sl, :] = (mine + passing[i, passing_rows(n), :].astype(F32)).astype(BF16)
            scatter_copy(4 + i, part, arrived, passing, n).start()

    def scatter_end(share, part, arrived, passing, n, result):
        for e, waits in ((1, (2, 5)), (0, (3, 4))):
            sl = pl.ds(*pieces(n)[e])
            mine = share(t, sl)
            for i in waits:
                scatter_copy(i, part, arrived, passing, n).wait_recv()
            result[sl, :] = (
                mine + arrived[0, sl, :].astype(F32) + arrived[1, sl, :].astype(F32)
            ).astype(BF16)
        for i in range(6):
            scatter_copy(i, part, arrived, passing, n).wait_send()

    def out_share(slot, sl):
        return nn(at[sl, :], wo[slot])

    scatter_early(out_share, p_out, v_out, f_out, 0)

    for hf in range(2):
        sl = pl.ds(hf * HALF, HALF)
        for u in (4 + 2 * hf, 5 + 2 * hf):
            forward(u).wait_recv()
        g = (gacc[sl, :] + nt(gr[1, sl, :], wo[opp])).astype(BF16)
        for h in range(HEADS):
            part = g[:, h * HEAD : (h + 1) * HEAD]
            gn[h, sl, :] = part
            gt[:, pl.ds(h * ROWS + hf * HALF, HALF)] = part.T
    delta[...] = jnp.sum(gt[...].astype(F32) * att[...].astype(F32), axis=0, keepdims=True)
    oacc[...] = jnp.zeros(oacc.shape, F32)

    def dkv_sibling(d, hf):
        return remote(sib_out.at[d, hf], sib_in.at[d, hf], dss.at[d, hf], dsr.at[d, hf], sibling)

    def dkv_send(d, hf):
        return remote(
            dkv_out.at[d - 1, hf], dkv_in.at[d - 1, hf], dos.at[d - 1, hf], dor.at[d - 1, hf],
            {"seq": s - 2 * d, "tp": t},
        )

    def backward(d, hf):
        both = kv[chip - d, :, hf].reshape(2 * HALF, 2 * HEAD)
        k, v = both[:, :HEAD], both[:, HEAD:]
        kt = k.T
        key = key_at + ((chip - d) * (4 * HALF) + hf * HALF)
        allowed = (key >= first_key) & (key <= row_index)
        following = (nn(k, qt[:, :ROWS]), nn(v, gt[:, :ROWS]))
        held = None
        dk = jnp.zeros((2 * HALF, HEAD), F32)
        dv = jnp.zeros((2 * HALF, HEAD), F32)
        for h in range(HEADS + 1):
            sl = slice(h * ROWS, (h + 1) * ROWS)
            raw, dprob = following
            if h + 1 < HEADS:
                nxt = slice((h + 1) * ROWS, (h + 2) * ROWS)
                following = (nn(k, qt[:, nxt]), nn(v, gt[:, nxt]))
            if held is not None:
                cols, prob_b, ds_b = held
                dv = dv + nn(prob_b, gn[h - 1])
                dk = dk + nn(ds_b, qn[h - 1])
                oacc[:, cols] = oacc[:, cols] + nn(kt, ds_b)
            if h < HEADS:
                prob = jnp.where(allowed, jnp.exp2(raw * scale - lse[:, sl]), 0.0)
                ds = prob * (dprob - delta[:, sl])
                held = (sl, prob.astype(BF16), ds.astype(BF16))
        tmp[:, :, :HEAD] = (dk * factor).reshape(2, HALF, HEAD)
        tmp[:, :, HEAD:] = dv.reshape(2, HALF, HEAD)
        own[d, hf] = tmp[core]
        sib_out[d, hf] = tmp[1 - core].astype(BF16)
        dkv_sibling(d, hf).start()

    span = REACH + 1

    def dkv_pump(i):
        d, hf = REACH - lax.rem(i, span), lax.div(i, span)

        @pl.when((chip >= d) & (d > 0))
        def _():
            dkv_sibling(d, hf).wait_recv()
            dkv_out[d - 1, hf] = (own[d, hf] + sib_in[d, hf].astype(F32)).astype(BF16)
            dkv_send(d, hf).start()

    def backward_step(i, carry):
        d, hf = REACH - lax.rem(i, span), lax.div(i, span)

        @pl.when(chip >= d)
        def _():
            backward(d, hf)

        @pl.when(i > 0)
        def _():
            dkv_pump(i - 1)

        @pl.when(i == span - 1)
        def _():
            scatter_late(out_share, p_out, v_out, f_out, 0)

        return carry

    lax.fori_loop(0, 2 * span, backward_step, 0)
    for h in range(HEADS):
        u = oacc[:, h * ROWS : (h + 1) * ROWS].T * factor
        x[:, h * HEAD : (h + 1) * HEAD] = (
            u * cos_ref[...] - pltpu.roll(u, HEAD // 2, 1) * sin_ref[...]
        ).astype(BF16)
    def finish_pair(hf):
        dkv_sibling(0, hf).wait_recv()
        own[0, hf] = own[0, hf] + sib_in[0, hf].astype(F32)
        for d in range(1, REACH + 1):
            @pl.when(chip + d < CHIPS)
            def _():
                dkv_send(d, hf).wait_recv()
                own[0, hf] = own[0, hf] + dkv_in[d - 1, hf].astype(F32)
        sl = pl.ds(hf * HALF, HALF)
        u = own[0, hf, :, :HEAD]
        x[sl, FEAT : FEAT + HEAD] = (
            u * cos_ref[sl, :] - pltpu.roll(u, HEAD // 2, 1) * sin_ref[sl, :]
        ).astype(BF16)
        x[sl, FEAT + HEAD :] = own[0, hf, :, HEAD:].astype(BF16)

    def grad_share(slot, sl):
        return nt(x[sl, :], w[slot])

    finish_pair(0)
    scatter_early(grad_share, p_grad, v_grad, f_grad, 1)
    scatter_end(out_share, p_out, v_out, f_out, 0, out_ref)
    scatter_late(grad_share, p_grad, v_grad, f_grad, 1)
    finish_pair(1)
    scatter_early(grad_share, p_grad, v_grad, f_grad, 2)
    scatter_end(grad_share, p_grad, v_grad, f_grad, 1, gtok_ref)
    scatter_late(grad_share, p_grad, v_grad, f_grad, 2)

    for u in range(8):
        for way in range(2):
            send(u, way).wait_send()
        forward(u).wait_send()
    for hf in range(2):
        for j in range(1, 16):
            kv_copy(hf, j // 4, j % 4).wait_send()
        for d in range(REACH + 1):
            @pl.when(chip >= d)
            def _():
                kv_sibling(d, hf).wait_send()
                dkv_sibling(d, hf).wait_send()
                if d > 0:
                    dkv_send(d, hf).wait_send()
    scatter_end(grad_share, p_grad, v_grad, f_grad, 2, gtok_ref)


def local(
    tokens, w_query, b_query, w_key, key_bias, value_weight, value_bias, w_out, doc_lengths, grad_out
):
    freq = theta_base ** (-2.0 * np.arange(HEAD // 2) / HEAD)
    freq = jnp.asarray(np.concatenate([freq, freq])[None, :], F32)
    vm = pl.BlockSpec(memory_space=pltpu.VMEM)
    hbm = pl.BlockSpec(memory_space=pl.ANY)
    dma = pltpu.SemaphoreType.DMA
    shape = jax.ShapeDtypeStruct((ROWS, WIDTH), BF16)
    results = pl.pallas_call(
        block_kernel,
        out_shape=(shape, shape),
        in_specs=[pl.BlockSpec(memory_space=pltpu.SMEM), vm, vm, hbm, hbm, hbm, hbm, vm, vm, vm, vm],
        out_specs=(vm, vm),
        scratch_shapes=[
            pltpu.VMEM((ROWS, HEAD), F32),
            pltpu.VMEM((ROWS, HEAD), F32),
            pltpu.VMEM((4, WIDTH, FEAT + 2 * HEAD), BF16),
            pltpu.VMEM((4, FEAT, WIDTH), BF16),
            pltpu.VMEM((3, ROWS, WIDTH), BF16),
            pltpu.VMEM((3, ROWS, WIDTH), BF16),
            pltpu.VMEM((ROWS, FEAT + 2 * HEAD), F32),
            pltpu.VMEM((ROWS, FEAT), F32),
            pltpu.VMEM((HEADS, ROWS, HEAD), BF16),
            pltpu.VMEM((HEAD, HEADS * ROWS), BF16),
            pltpu.VMEM((HEADS, ROWS, HEAD), BF16),
            pltpu.VMEM((HEAD, HEADS * ROWS), BF16),
            pltpu.VMEM((CHIPS, 2, 2, HALF, 2 * HEAD), BF16),
            pltpu.VMEM((ROWS, FEAT), BF16),
            pltpu.VMEM((HEAD, HEADS * ROWS), BF16),
            pltpu.VMEM((HEAD, HEADS * ROWS), F32),
            pltpu.VMEM((1, HEADS * ROWS), F32),
            pltpu.VMEM((1, HEADS * ROWS), F32),
            pltpu.VMEM((1, HEADS * ROWS), F32),
            pltpu.VMEM((1, HEADS * ROWS), F32),
            pltpu.VMEM((2, HALF, 2 * HEAD), F32),
            pltpu.VMEM((REACH + 1, 2, HALF, 2 * HEAD), F32),
            pltpu.VMEM((REACH + 1, 2, HALF, 2 * HEAD), BF16),
            pltpu.VMEM((REACH + 1, 2, HALF, 2 * HEAD), BF16),
            pltpu.VMEM((REACH, 2, HALF, 2 * HEAD), BF16),
            pltpu.VMEM((REACH, 2, HALF, 2 * HEAD), BF16),
            pltpu.VMEM((ROWS, FEAT + 2 * HEAD), BF16),
            pltpu.VMEM((3, ROWS, WIDTH), BF16),
            pltpu.VMEM((2, ROWS, WIDTH), BF16),
            pltpu.VMEM((2, HALF, WIDTH), BF16),
            pltpu.VMEM((3, ROWS, WIDTH), BF16),
            pltpu.VMEM((2, ROWS, WIDTH), BF16),
            pltpu.VMEM((2, HALF, WIDTH), BF16),
            dma((16,)),
            dma((8, 2)), dma((8, 2)),
            dma((8,)), dma((8,)),
            dma((2, 4, 4)), dma((2, 4, 4)),
            dma((REACH + 1, 2)), dma((REACH + 1, 2)),
            dma((REACH + 1, 2)), dma((REACH + 1, 2)),
            dma((REACH, 2)), dma((REACH, 2)),
            dma((3, 6)), dma((3, 6)),
        ],
        compiler_params=pltpu.CompilerParams(
            collective_id=0, has_side_effects=True, vmem_limit_bytes=60 << 20
        ),
        name="attention_block",
    )(
        doc_lengths, tokens, grad_out, w_query, w_key, value_weight, w_out,
        b_query[None, :], key_bias[None, :], value_bias[None, :], freq,
    )
    return results


def solution(mesh):
    return jax.shard_map(
        local,
        mesh=mesh,
        in_specs=(
            P("seq", "tp"),
            P(None, "tp"),
            P("tp"),
            P(None, "tp"),
            P("tp"),
            P(None, "tp"),
            P("tp"),
            P("tp", None),
            P(),
            P("seq", "tp"),
        ),
        out_specs=(P("seq", "tp"), P("seq", "tp")),
        check_vma=False,
    )
```

```python
import functools

import jax
import jax.numpy as jnp
import numpy as np
from jax import lax
from jax.experimental import pallas as pl
from jax.experimental.pallas import tpu as pltpu
from jax.sharding import PartitionSpec as P

theta_base = 1000000.0
neg_large = -1e30
log2e = 1.4426950408889634
HEAD = 128
ROWS = 256
HALF = 128
CHUNK = 64
HEADS = 5
WIDTH = 1280
FEAT = HEADS * HEAD
CHIPS = 16
REACH = 8
F32 = jnp.float32
BF16 = jnp.bfloat16
MESH = pl.DeviceIdType.MESH
factor = HEAD**-0.5
scale = factor * log2e


def nn(a, b):
    return lax.dot_general(a, b, (((1,), (0,)), ((), ())), preferred_element_type=F32)


def nt(a, b):
    return lax.dot_general(a, b, (((1,), (1,)), ((), ())), preferred_element_type=F32)


def block_kernel(
    lengths, tok, grad, wq_hbm, wk_hbm, wv_hbm, wo_hbm, bq, bk, bv, freq_ref,
    out_ref, gtok_ref,
    cos_ref, sin_ref, w, wo, tk, gr, acc, gacc, qn, qt, gn, gt, kv, at, att, oacc, m_s, l_s, lse, delta,
    tmp, own, sib_out, sib_in, dkv_out, dkv_in, x, p_out, v_out, f_out, p_grad, v_grad, f_grad, kept,
    wsem, ys, yr, fs, fr, kvs, kvr, sbs, sbr, dss, dsr, dos, dor, rss, rsr,
):
    s = lax.axis_index("seq")
    t = lax.axis_index("tp")
    chip, core = lax.div(s, 2), lax.rem(s, 2)
    right, left, opp = lax.rem(t + 1, 4), lax.rem(t + 3, 4), lax.rem(t + 2, 4)
    to_right, to_left = {"seq": s, "tp": right}, {"seq": s, "tp": left}
    sibling = {"seq": s + 1 - 2 * core, "tp": t}
    at_z, at_x = lax.div(chip, 4), lax.rem(chip, 4)
    m1 = at_x + core * (at_z - at_x)
    m2 = at_z + core * (at_x - at_z)
    stride1, stride2 = 1 + 3 * core, 4 - 3 * core

    def place(r2, r1):
        return lax.rem(m1 + 4 - r1, 4) * stride1 + lax.rem(m2 + 4 - r2, 4) * stride2

    def towards(step2, step1):
        return {"seq": 2 * place(-step2, -step1) + core, "tp": t}

    up1, down1, up2, down2 = towards(0, 1), towards(0, -1), towards(1, 0), towards(-1, 0)
    across1 = towards(0, 2)

    def remote(src, dst, send, recv, device):
        return pltpu.make_async_remote_copy(
            src_ref=src, dst_ref=dst, send_sem=send, recv_sem=recv,
            device_id=device, device_id_type=MESH,
        )

    loads = []
    for i in range(4):
        for j, (ref, lo, hi) in enumerate(
            ((wq_hbm, 0, FEAT), (wk_hbm, FEAT, FEAT + HEAD), (wv_hbm, FEAT + HEAD, FEAT + 2 * HEAD))
        ):
            loads.append(
                pltpu.make_async_copy(
                    ref.at[pl.ds(i * WIDTH, WIDTH)], w.at[i, :, lo:hi], wsem.at[3 * i + j]
                )
            )
    loads_out = [
        pltpu.make_async_copy(wo_hbm.at[:, pl.ds(i * WIDTH, WIDTH)], wo.at[i], wsem.at[12 + i])
        for i in range(4)
    ]
    for copy in loads + loads_out:
        copy.start()

    barrier = pltpu.get_barrier_semaphore()
    partners = (to_right, to_left, sibling, up1, down1, up2, down2, across1)
    for device in partners:
        pl.semaphore_signal(barrier, inc=1, device_id=device, device_id_type=MESH)
    for d in range(1, REACH + 1):
        @pl.when(chip + d < CHIPS)
        def _():
            pl.semaphore_signal(
                barrier, inc=1, device_id={"seq": s + 2 * d, "tp": t}, device_id_type=MESH
            )

        @pl.when(chip >= d)
        def _():
            pl.semaphore_signal(
                barrier, inc=1, device_id={"seq": s - 2 * d, "tp": t}, device_id_type=MESH
            )
    pl.semaphore_wait(
        barrier,
        len(partners) + jnp.minimum(chip, REACH) + jnp.minimum(CHIPS - 1 - chip, REACH),
    )

    def unit(u):
        src, buf = (tok, tk) if u < 4 else (grad, gr)
        return src, buf, pl.ds((u % 4) * CHUNK, CHUNK)

    def send(u, way):
        src, buf, sl = unit(u)
        if way == 0:
            return remote(src.at[sl], buf.at[0, sl], ys.at[u, 0], yr.at[u, 0], to_right)
        return remote(src.at[sl], buf.at[2, sl], ys.at[u, 1], yr.at[u, 1], to_left)

    def forward(u, way):
        _, buf, _ = unit(u)
        sl = pl.ds((u % 4) * CHUNK + way * (CHUNK // 2), CHUNK // 2)
        return remote(
            buf.at[2 * way, sl], buf.at[1, sl], fs.at[u, way], fr.at[u, way],
            to_left if way else to_right,
        )

    def issue(u):
        for way in range(2):
            send(u, way).start()

    def pump(u):
        for way in range(2):
            send(u, way).wait_recv()
            forward(u, way).start()

    def passed(u):
        for way in range(2):
            forward(u, way).wait_recv()

    def kv_copy(hf, r2, r1):
        if r2 == 0:
            src = (0, 0)
            device = (up1, across1, down1)[r1 - 1]
        elif r2 == 2:
            src, device = ((1, r1), up2) if r1 < 2 else ((3, r1), down2)
        else:
            src, device = (0, r1), up2 if r2 == 1 else down2
        here = kv.at[place(*src), core, hf]
        return remote(here, here, kvs.at[hf, r2, r1], kvr.at[hf, r2, r1], device)

    def kv_start(hf, *slots):
        for slot in slots:
            kv_copy(hf, *slot).start()

    def kv_wait(hf, *slots):
        for r2, r1 in slots:
            there = kv.at[place(r2, r1), core, hf]
            remote(there, there, kvs.at[hf, r2, r1], kvr.at[hf, r2, r1], sibling).wait_recv()

    def kv_second(hf):
        kv_wait(hf, (1, 0))
        kv_start(hf, (2, 0))
        for r1 in (1, 3, 2):
            kv_wait(hf, (0, r1))
            kv_start(hf, (1, r1), (3, r1))

    def kv_third(hf):
        kv_wait(hf, (1, 1))
        kv_start(hf, (2, 1))
        kv_wait(hf, (3, 3))
        kv_start(hf, (2, 3))
        kv_wait(hf, (3, 2))
        kv_start(hf, (2, 2))

    def kv_fifth(hf):
        kv_wait(hf, (1, 2), (1, 3), (3, 0), (3, 1), (2, 0), (2, 1), (2, 2), (2, 3))
        for d in range(1, REACH + 1):
            @pl.when(chip >= d)
            def _():
                kv_sibling(d, hf).start()

    def kv_sibling(d, hf):
        there = kv.at[chip - d, core, hf]
        return remote(there, there, sbs.at[d, hf], sbr.at[d, hf], sibling)

    def make_rows(hf):
        sl = pl.ds(hf * HALF, HALF)
        cos, sin = cos_ref[sl, :], sin_ref[sl, :]

        def rotated(i):
            u = acc[sl, i * HEAD : (i + 1) * HEAD]
            u = u + (bq[i * HEAD : (i + 1) * HEAD] if i < HEADS else bk[...]).astype(F32)
            return (u * cos + pltpu.roll(u, HEAD // 2, 1) * sin).astype(BF16)

        kv[chip, core, hf, :, :HEAD] = rotated(HEADS)
        kv[chip, core, hf, :, HEAD:] = (
            acc[sl, (HEADS + 1) * HEAD :] + bv[...].astype(F32)
        ).astype(BF16)
        kv_start(hf, (0, 1), (0, 3), (1, 0), (3, 0), (0, 2))
        kv_sibling(0, hf).start()
        for h in range(HEADS):
            q = rotated(h)
            qn[h, sl, :] = q
            qt[:, pl.ds(h * ROWS + hf * HALF, HALF)] = q.T

    for u in range(4):
        issue(u)
    end0 = lengths[0]
    end1 = end0 + lengths[1]
    end2 = end1 + lengths[2]

    def start_at(index):
        later = jnp.where(index >= end2, end2, jnp.where(index >= end1, end1, end0))
        return jnp.where(index >= end0, later, 0)

    row_index = s * ROWS + lax.broadcasted_iota(jnp.int32, (1, ROWS), 1)
    first_key = start_at(row_index)
    index = s * ROWS + lax.broadcasted_iota(jnp.int32, (ROWS, HEAD), 0)
    angles = (index - start_at(index)).astype(F32) * freq_ref[...]
    cos_ref[...] = jnp.cos(angles)
    sine = jnp.sin(angles)
    lane = lax.broadcasted_iota(jnp.int32, (ROWS, HEAD), 1)
    sin_ref[...] = jnp.where(lane < HEAD // 2, -sine, sine)

    for copy in loads:
        copy.wait()
    acc[...] = nn(tok[...], w[t])
    pump(0)
    for copy in loads_out:
        copy.wait()
    gacc[...] = nt(grad[...], wo[t])
    m_s[...] = jnp.full(m_s.shape, neg_large, F32)
    l_s[...] = jnp.zeros(l_s.shape, F32)
    oacc[...] = jnp.zeros(oacc.shape, F32)
    pump(1)
    halves = [pl.ds(hf * HALF, HALF) for hf in range(2)]
    for hf, sl in enumerate(halves):
        if hf == 1:
            pump(2)
            pump(3)
            for u in range(4, 7):
                issue(u)
        acc[sl, :] += nn(tk[0, sl, :], w[left])
        acc[sl, :] += nn(tk[2, sl, :], w[right])
    for hf, sl in enumerate(halves):
        for u in (2 * hf, 2 * hf + 1):
            passed(u)
        acc[sl, :] += nn(tk[1, sl, :], w[opp])
        make_rows(hf)

    r2 = lax.broadcasted_iota(jnp.int32, (2 * HALF, ROWS), 0)
    key_at = jnp.where(r2 >= HALF, r2 + HALF, r2)

    def attend(first, second):
        both = jnp.concatenate(
            [kv[jnp.maximum(c, 0), :, hf].reshape(2 * HALF, 2 * HEAD) for c, hf in (first, second)],
            axis=0,
        )
        k = both[:, :HEAD]
        vt = both[:, HEAD:].T
        key = jnp.concatenate(
            [key_at + (c * (4 * HALF) + hf * HALF) for c, hf in (first, second)], axis=0
        )
        allowed = (key >= first_key) & (key <= row_index)
        following = nn(k, qt[:, :ROWS])
        held = None
        for h in range(HEADS + 1):
            sl = slice(h * ROWS, (h + 1) * ROWS)
            raw = following
            if h + 1 < HEADS:
                following = nn(k, qt[:, (h + 1) * ROWS : (h + 2) * ROWS])
            if held is not None:
                cols, weights, shrink = held
                oacc[:, cols] = oacc[:, cols] * shrink + nn(vt, weights)
            if h < HEADS:
                scores = jnp.where(allowed, raw * scale, neg_large)
                old = m_s[:, sl]
                top = jnp.maximum(old, jnp.max(scores, axis=0, keepdims=True))
                weights = jnp.exp2(scores - top)
                shrink = jnp.exp2(old - top)
                l_s[:, sl] = l_s[:, sl] * shrink + jnp.sum(weights, axis=0, keepdims=True)
                m_s[:, sl] = top
                held = (sl, weights.astype(BF16), shrink)

    def gather_grad(hf):
        sl = halves[hf]
        gacc[sl, :] += nt(gr[0, sl, :], wo[left])
        gacc[sl, :] += nt(gr[2, sl, :], wo[right])

    def forward_step(i, carry):
        j, hf = lax.rem(i + 3, 4), lax.div(i + 3, 4) - 1
        d = 2 * j + 1
        is_own = i == 0

        @pl.when(i == 1)
        def _():
            pump(5)
            gather_grad(0)
            kv_third(1)
            kv_fifth(0)

        @pl.when(i == 2)
        def _():
            pump(6)

        @pl.when(i == 4)
        def _():
            pump(7)

        @pl.when(i == 5)
        def _():
            kv_fifth(1)
            gather_grad(1)

        for e in range(2):
            @pl.when((i > 0) & (chip >= d + e))
            def _():
                kv_sibling(d + e, hf).wait_recv()

        @pl.when(is_own | (chip >= d))
        def _():
            attend(
                (jnp.where(is_own, chip, chip - d), jnp.where(is_own, 0, hf)),
                (jnp.where(is_own, chip, chip - d - 1), jnp.where(is_own, 1, hf)),
            )

        return carry

    issue(7)
    kv_second(0)
    kv_second(1)
    kv_third(0)
    pump(4)
    for hf in range(2):
        kv_sibling(0, hf).wait_recv()
    lax.fori_loop(0, REACH + 1, forward_step, 0)
    for h in range(HEADS):
        sl = slice(h * ROWS, (h + 1) * ROWS)
        mass = l_s[:, sl]
        o = (oacc[:, sl] / mass).astype(BF16)
        att[:, sl] = o
        at[:, h * HEAD : (h + 1) * HEAD] = o.T
        lse[:, sl] = m_s[:, sl] + jnp.log2(mass)

    def pieces(n):
        return ((0, HALF), (HALF, HALF)) if n == 0 else (
            ((n - 1) * HALF, CHUNK), ((n - 1) * HALF + CHUNK, CHUNK)
        )

    def passing_rows(n):
        return pl.ds(0, HALF) if n == 0 else pl.ds((n - 1) * CHUNK, CHUNK)

    def scatter_copy(i, part, arrived, passing, n):
        a, b = [pl.ds(*piece) for piece in pieces(n)]
        over = passing_rows(n)
        src, dst, device = (
            (part.at[1, a], passing.at[0, over], to_right),
            (part.at[1, b], passing.at[1, over], to_left),
            (part.at[2, b], arrived.at[0, b], to_right),
            (part.at[0, a], arrived.at[1, a], to_left),
            (part.at[2, a], arrived.at[0, a], to_right),
            (part.at[0, b], arrived.at[1, b], to_left),
        )[i]
        return remote(src, dst, rss.at[n, i], rsr.at[n, i], device)

    def scatter_early(share, part, arrived, passing, n):
        (first, rows), (second, _) = pieces(n)
        both = pl.ds(first, 2 * rows)
        part[1, both, :] = share(opp, both).astype(BF16)
        for i in range(2):
            scatter_copy(i, part, arrived, passing, n).start()
        mine = share(right, both)
        part[2, pl.ds(second, rows), :] = mine[rows:].astype(BF16)
        scatter_copy(2, part, arrived, passing, n).start()
        kept[0, pl.ds(0, rows), :] = mine[:rows]
        mine = share(left, both)
        part[0, pl.ds(first, rows), :] = mine[:rows].astype(BF16)
        scatter_copy(3, part, arrived, passing, n).start()
        kept[1, pl.ds(0, rows), :] = mine[rows:]

    def scatter_late(part, arrived, passing, n):
        for i, rel in ((0, 2), (1, 0)):
            base, rows = pieces(n)[i]
            scatter_copy(i, part, arrived, passing, n).wait_recv()
            part[rel, pl.ds(base, rows), :] = (
                kept[i, pl.ds(0, rows), :] + passing[i, passing_rows(n), :].astype(F32)
            ).astype(BF16)
            scatter_copy(4 + i, part, arrived, passing, n).start()

    def scatter_end(share, part, arrived, passing, n, result):
        (first, rows), _ = pieces(n)
        both = pl.ds(first, 2 * rows)
        mine = share(t, both)
        for i in range(2, 6):
            scatter_copy(i, part, arrived, passing, n).wait_recv()
        result[both, :] = (
            mine + arrived[0, both, :].astype(F32) + arrived[1, both, :].astype(F32)
        ).astype(BF16)
        for i in range(6):
            scatter_copy(i, part, arrived, passing, n).wait_send()

    def out_share(slot, sl):
        return nn(at[sl, :], wo[slot])

    scatter_early(out_share, p_out, v_out, f_out, 0)

    for hf in range(2):
        sl = pl.ds(hf * HALF, HALF)
        for u in (4 + 2 * hf, 5 + 2 * hf):
            passed(u)
        g = (gacc[sl, :] + nt(gr[1, sl, :], wo[opp])).astype(BF16)
        for h in range(HEADS):
            part = g[:, h * HEAD : (h + 1) * HEAD]
            gn[h, sl, :] = part
            gt[:, pl.ds(h * ROWS + hf * HALF, HALF)] = part.T
    delta[...] = jnp.sum(gt[...].astype(F32) * att[...].astype(F32), axis=0, keepdims=True)
    oacc[...] = jnp.zeros(oacc.shape, F32)

    def dkv_sibling(d, hf):
        return remote(sib_out.at[d, hf], sib_in.at[d, hf], dss.at[d, hf], dsr.at[d, hf], sibling)

    def dkv_send(d, hf):
        return remote(
            dkv_out.at[d - 1, hf], dkv_in.at[d - 1, hf], dos.at[d - 1, hf], dor.at[d - 1, hf],
            {"seq": s - 2 * d, "tp": t},
        )

    def backward(d, hf):
        both = kv[chip - d, :, hf].reshape(2 * HALF, 2 * HEAD)
        k, v = both[:, :HEAD], both[:, HEAD:]
        kt = k.T
        key = key_at + ((chip - d) * (4 * HALF) + hf * HALF)
        allowed = (key >= first_key) & (key <= row_index)
        following = (nn(k, qt[:, :ROWS]), nn(v, gt[:, :ROWS]))
        held = None
        dk = jnp.zeros((2 * HALF, HEAD), F32)
        dv = jnp.zeros((2 * HALF, HEAD), F32)
        for h in range(HEADS + 1):
            sl = slice(h * ROWS, (h + 1) * ROWS)
            raw, dprob = following
            if h + 1 < HEADS:
                nxt = slice((h + 1) * ROWS, (h + 2) * ROWS)
                following = (nn(k, qt[:, nxt]), nn(v, gt[:, nxt]))
            if held is not None:
                cols, prob_b, ds_b = held
                dv = dv + nn(prob_b, gn[h - 1])
                dk = dk + nn(ds_b, qn[h - 1])
                oacc[:, cols] = oacc[:, cols] + nn(kt, ds_b)
            if h < HEADS:
                prob = jnp.where(allowed, jnp.exp2(raw * scale - lse[:, sl]), 0.0)
                ds = prob * (dprob - delta[:, sl])
                held = (sl, prob.astype(BF16), ds.astype(BF16))
        tmp[:, :, :HEAD] = (dk * factor).reshape(2, HALF, HEAD)
        tmp[:, :, HEAD:] = dv.reshape(2, HALF, HEAD)
        own[d, hf] = tmp[core]
        sib_out[d, hf] = tmp[1 - core].astype(BF16)
        dkv_sibling(d, hf).start()

    span = REACH + 1

    def dkv_pump(i):
        d, hf = REACH - lax.rem(i, span), lax.div(i, span)

        @pl.when((chip >= d) & (d > 0))
        def _():
            dkv_sibling(d, hf).wait_recv()
            dkv_out[d - 1, hf] = (own[d, hf] + sib_in[d, hf].astype(F32)).astype(BF16)
            dkv_send(d, hf).start()

    def backward_step(i, carry):
        d, hf = REACH - lax.rem(i, span), lax.div(i, span)

        @pl.when(chip >= d)
        def _():
            backward(d, hf)

        @pl.when(i > 0)
        def _():
            dkv_pump(i - 1)

        @pl.when(i == span - 1)
        def _():
            scatter_late(p_out, v_out, f_out, 0)

        return carry

    lax.fori_loop(0, 2 * span, backward_step, 0)
    for h in range(HEADS):
        u = oacc[:, h * ROWS : (h + 1) * ROWS].T * factor
        x[:, h * HEAD : (h + 1) * HEAD] = (
            u * cos_ref[...] - pltpu.roll(u, HEAD // 2, 1) * sin_ref[...]
        ).astype(BF16)
    def finish_pair(hf):
        dkv_sibling(0, hf).wait_recv()
        own[0, hf] = own[0, hf] + sib_in[0, hf].astype(F32)
        for d in range(1, REACH + 1):
            @pl.when(chip + d < CHIPS)
            def _():
                dkv_send(d, hf).wait_recv()
                own[0, hf] = own[0, hf] + dkv_in[d - 1, hf].astype(F32)
        sl = pl.ds(hf * HALF, HALF)
        u = own[0, hf, :, :HEAD]
        x[sl, FEAT : FEAT + HEAD] = (
            u * cos_ref[sl, :] - pltpu.roll(u, HEAD // 2, 1) * sin_ref[sl, :]
        ).astype(BF16)
        x[sl, FEAT + HEAD :] = own[0, hf, :, HEAD:].astype(BF16)

    def grad_share(slot, sl):
        return nt(x[sl, :], w[slot])

    finish_pair(0)
    scatter_early(grad_share, p_grad, v_grad, f_grad, 1)
    scatter_end(out_share, p_out, v_out, f_out, 0, out_ref)
    scatter_late(p_grad, v_grad, f_grad, 1)
    finish_pair(1)
    scatter_early(grad_share, p_grad, v_grad, f_grad, 2)
    scatter_end(grad_share, p_grad, v_grad, f_grad, 1, gtok_ref)
    scatter_late(p_grad, v_grad, f_grad, 2)

    for u in range(8):
        for way in range(2):
            send(u, way).wait_send()
            forward(u, way).wait_send()
    for hf in range(2):
        for j in range(1, 16):
            kv_copy(hf, j // 4, j % 4).wait_send()
        for d in range(REACH + 1):
            @pl.when(chip >= d)
            def _():
                kv_sibling(d, hf).wait_send()
                dkv_sibling(d, hf).wait_send()
                if d > 0:
                    dkv_send(d, hf).wait_send()
    scatter_end(grad_share, p_grad, v_grad, f_grad, 2, gtok_ref)


def hand_over(a, b, c, d):
    c[...] = a[...]
    d[...] = b[...]


def local(
    tokens, w_query, b_query, w_key, key_bias, value_weight, value_bias, w_out, doc_lengths, grad_out
):
    freq = theta_base ** (-2.0 * np.arange(HEAD // 2) / HEAD)
    freq = jnp.asarray(np.concatenate([freq, freq])[None, :], F32)
    vm = pl.BlockSpec(memory_space=pltpu.VMEM)
    hbm = pl.BlockSpec(memory_space=pl.ANY)
    dma = pltpu.SemaphoreType.DMA
    shape = jax.ShapeDtypeStruct((ROWS, WIDTH), BF16)
    results = pl.pallas_call(
        block_kernel,
        out_shape=(shape, shape),
        in_specs=[pl.BlockSpec(memory_space=pltpu.SMEM), vm, vm, hbm, hbm, hbm, hbm, vm, vm, vm, vm],
        out_specs=(vm, vm),
        scratch_shapes=[
            pltpu.VMEM((ROWS, HEAD), F32),
            pltpu.VMEM((ROWS, HEAD), F32),
            pltpu.VMEM((4, WIDTH, FEAT + 2 * HEAD), BF16),
            pltpu.VMEM((4, FEAT, WIDTH), BF16),
            pltpu.VMEM((3, ROWS, WIDTH), BF16),
            pltpu.VMEM((3, ROWS, WIDTH), BF16),
            pltpu.VMEM((ROWS, FEAT + 2 * HEAD), F32),
            pltpu.VMEM((ROWS, FEAT), F32),
            pltpu.VMEM((HEADS, ROWS, HEAD), BF16),
            pltpu.VMEM((HEAD, HEADS * ROWS), BF16),
            pltpu.VMEM((HEADS, ROWS, HEAD), BF16),
            pltpu.VMEM((HEAD, HEADS * ROWS), BF16),
            pltpu.VMEM((CHIPS, 2, 2, HALF, 2 * HEAD), BF16),
            pltpu.VMEM((ROWS, FEAT), BF16),
            pltpu.VMEM((HEAD, HEADS * ROWS), BF16),
            pltpu.VMEM((HEAD, HEADS * ROWS), F32),
            pltpu.VMEM((1, HEADS * ROWS), F32),
            pltpu.VMEM((1, HEADS * ROWS), F32),
            pltpu.VMEM((1, HEADS * ROWS), F32),
            pltpu.VMEM((1, HEADS * ROWS), F32),
            pltpu.VMEM((2, HALF, 2 * HEAD), F32),
            pltpu.VMEM((REACH + 1, 2, HALF, 2 * HEAD), F32),
            pltpu.VMEM((REACH + 1, 2, HALF, 2 * HEAD), BF16),
            pltpu.VMEM((REACH + 1, 2, HALF, 2 * HEAD), BF16),
            pltpu.VMEM((REACH, 2, HALF, 2 * HEAD), BF16),
            pltpu.VMEM((REACH, 2, HALF, 2 * HEAD), BF16),
            pltpu.VMEM((ROWS, FEAT + 2 * HEAD), BF16),
            pltpu.VMEM((3, ROWS, WIDTH), BF16),
            pltpu.VMEM((2, ROWS, WIDTH), BF16),
            pltpu.VMEM((2, HALF, WIDTH), BF16),
            pltpu.VMEM((3, ROWS, WIDTH), BF16),
            pltpu.VMEM((2, ROWS, WIDTH), BF16),
            pltpu.VMEM((2, HALF, WIDTH), BF16),
            pltpu.VMEM((2, HALF, WIDTH), F32),
            dma((16,)),
            dma((8, 2)), dma((8, 2)),
            dma((8, 2)), dma((8, 2)),
            dma((2, 4, 4)), dma((2, 4, 4)),
            dma((REACH + 1, 2)), dma((REACH + 1, 2)),
            dma((REACH + 1, 2)), dma((REACH + 1, 2)),
            dma((REACH, 2)), dma((REACH, 2)),
            dma((3, 6)), dma((3, 6)),
        ],
        compiler_params=pltpu.CompilerParams(
            collective_id=0, has_side_effects=True, vmem_limit_bytes=60 << 20
        ),
        name="attention_block",
    )(
        doc_lengths, tokens, grad_out, w_query, w_key, value_weight, w_out,
        b_query, key_bias, value_bias, freq,
    )
    return pl.pallas_call(
        hand_over,
        out_shape=(shape, shape),
        in_specs=[vm, vm],
        out_specs=(vm, vm),
        name="hand_over",
    )(*results)


def solution(mesh):
    return jax.shard_map(
        local,
        mesh=mesh,
        in_specs=(
            P("seq", "tp"),
            P(None, "tp"),
            P("tp"),
            P(None, "tp"),
            P("tp"),
            P(None, "tp"),
            P("tp"),
            P("tp", None),
            P(),
            P("seq", "tp"),
        ),
        out_specs=(P("seq", "tp"), P("seq", "tp")),
        check_vma=False,
    )
```

```python
import functools

import jax
import jax.numpy as jnp
import numpy as np
from jax import lax
from jax.experimental import pallas as pl
from jax.experimental.pallas import tpu as pltpu
from jax.sharding import PartitionSpec as P

theta_base = 1000000.0
neg_large = -1e30
log2e = 1.4426950408889634
HEAD = 128
ROWS = 256
HALF = 128
CHUNK = 64
HEADS = 5
WIDTH = 1280
FEAT = HEADS * HEAD
CHIPS = 16
REACH = 8
F32 = jnp.float32
BF16 = jnp.bfloat16
MESH = pl.DeviceIdType.MESH
factor = HEAD**-0.5
scale = factor * log2e


def nn(a, b):
    return lax.dot_general(a, b, (((1,), (0,)), ((), ())), preferred_element_type=F32)


def nt(a, b):
    return lax.dot_general(a, b, (((1,), (1,)), ((), ())), preferred_element_type=F32)


def block_kernel(
    lengths, tok, grad, wq_hbm, wk_hbm, wv_hbm, wo_hbm, bq, bk, bv, freq_ref,
    out_ref, gtok_ref,
    cos_ref, sin_ref, w, wo, tk, gr, acc, gacc, qn, qt, gn, gt, kv, at, att, oacc, m_s, l_s, lse, delta,
    tmp, own, sib_out, sib_in, dkv_out, dkv_in, x, p_out, v_out, f_out, p_grad, v_grad, f_grad, kept,
    wsem, ys, yr, fs, fr, kvs, kvr, sbs, sbr, dss, dsr, dos, dor, rss, rsr,
):
    s = lax.axis_index("seq")
    t = lax.axis_index("tp")
    chip, core = lax.div(s, 2), lax.rem(s, 2)
    right, left, opp = lax.rem(t + 1, 4), lax.rem(t + 3, 4), lax.rem(t + 2, 4)
    to_right, to_left = {"seq": s, "tp": right}, {"seq": s, "tp": left}
    sibling = {"seq": s + 1 - 2 * core, "tp": t}
    at_z, at_x = lax.div(chip, 4), lax.rem(chip, 4)
    m1 = at_x + core * (at_z - at_x)
    m2 = at_z + core * (at_x - at_z)
    stride1, stride2 = 1 + 3 * core, 4 - 3 * core

    def place(r2, r1):
        return lax.rem(m1 + 4 - r1, 4) * stride1 + lax.rem(m2 + 4 - r2, 4) * stride2

    def towards(step2, step1):
        return {"seq": 2 * place(-step2, -step1) + core, "tp": t}

    up1, down1, up2, down2 = towards(0, 1), towards(0, -1), towards(1, 0), towards(-1, 0)
    across1 = towards(0, 2)

    def remote(src, dst, send, recv, device):
        return pltpu.make_async_remote_copy(
            src_ref=src, dst_ref=dst, send_sem=send, recv_sem=recv,
            device_id=device, device_id_type=MESH,
        )

    loads = []
    for i in range(4):
        for j, (ref, lo, hi) in enumerate(
            ((wq_hbm, 0, FEAT), (wk_hbm, FEAT, FEAT + HEAD), (wv_hbm, FEAT + HEAD, FEAT + 2 * HEAD))
        ):
            loads.append(
                pltpu.make_async_copy(
                    ref.at[pl.ds(i * WIDTH, WIDTH)], w.at[i, :, lo:hi], wsem.at[3 * i + j]
                )
            )
    loads_out = [
        pltpu.make_async_copy(wo_hbm.at[:, pl.ds(i * WIDTH, WIDTH)], wo.at[i], wsem.at[12 + i])
        for i in range(4)
    ]
    for copy in loads + loads_out:
        copy.start()

    barrier = pltpu.get_barrier_semaphore()
    partners = (to_right, to_left, sibling, up1, down1, up2, down2, across1)
    for device in partners:
        pl.semaphore_signal(barrier, inc=1, device_id=device, device_id_type=MESH)
    for d in range(1, REACH + 1):
        @pl.when(chip + d < CHIPS)
        def _():
            pl.semaphore_signal(
                barrier, inc=1, device_id={"seq": s + 2 * d, "tp": t}, device_id_type=MESH
            )

        @pl.when(chip >= d)
        def _():
            pl.semaphore_signal(
                barrier, inc=1, device_id={"seq": s - 2 * d, "tp": t}, device_id_type=MESH
            )
    pl.semaphore_wait(
        barrier,
        len(partners) + jnp.minimum(chip, REACH) + jnp.minimum(CHIPS - 1 - chip, REACH),
    )

    def unit(u):
        src, buf = (tok, tk) if u < 4 else (grad, gr)
        return src, buf, pl.ds((u % 4) * CHUNK, CHUNK)

    def send(u, way):
        src, buf, sl = unit(u)
        if way == 0:
            return remote(src.at[sl], buf.at[0, sl], ys.at[u, 0], yr.at[u, 0], to_right)
        return remote(src.at[sl], buf.at[2, sl], ys.at[u, 1], yr.at[u, 1], to_left)

    def forward(u, way):
        _, buf, _ = unit(u)
        sl = pl.ds((u % 4) * CHUNK + way * (CHUNK // 2), CHUNK // 2)
        return remote(
            buf.at[2 * way, sl], buf.at[1, sl], fs.at[u, way], fr.at[u, way],
            to_left if way else to_right,
        )

    def issue(u):
        for way in range(2):
            send(u, way).start()

    def pump(u):
        for way in range(2):
            send(u, way).wait_recv()
            forward(u, way).start()

    def passed(u):
        for way in range(2):
            forward(u, way).wait_recv()

    def kv_copy(hf, r2, r1):
        if r2 == 0:
            src = (0, 0)
            device = (up1, across1, down1)[r1 - 1]
        elif r2 == 2:
            src, device = ((1, r1), up2) if r1 < 2 else ((3, r1), down2)
        else:
            src, device = (0, r1), up2 if r2 == 1 else down2
        here = kv.at[place(*src), core, hf]
        return remote(here, here, kvs.at[hf, r2, r1], kvr.at[hf, r2, r1], device)

    def kv_start(hf, *slots):
        for slot in slots:
            kv_copy(hf, *slot).start()

    def kv_wait(hf, *slots):
        for r2, r1 in slots:
            there = kv.at[place(r2, r1), core, hf]
            remote(there, there, kvs.at[hf, r2, r1], kvr.at[hf, r2, r1], sibling).wait_recv()

    def kv_second(hf):
        kv_wait(hf, (1, 0))
        kv_start(hf, (2, 0))
        for r1 in (1, 3, 2):
            kv_wait(hf, (0, r1))
            kv_start(hf, (1, r1), (3, r1))

    def kv_third(hf):
        kv_wait(hf, (1, 1))
        kv_start(hf, (2, 1))
        kv_wait(hf, (3, 3))
        kv_start(hf, (2, 3))
        kv_wait(hf, (3, 2))
        kv_start(hf, (2, 2))

    relayed = ((0, 1), (0, 2), (0, 3), (1, 0), (1, 1), (3, 2), (3, 3))

    def kv_need(hf, *distances):
        for d in distances:
            @pl.when(chip >= d)
            def _():
                back_z = at_z - lax.div(chip - d, 4)
                back_x = lax.rem(at_x + 4 - lax.rem(chip - d, 4), 4)
                r1 = back_x + core * (back_z - back_x)
                r2 = back_z + core * (back_x - back_z)
                waited = (r2 == 0) | ((r2 == 1) & (r1 < 2)) | ((r2 == 3) & (r1 >= 2))

                @pl.when(jnp.logical_not(waited))
                def _():
                    kv_wait(hf, (r2, r1))

                kv_sibling(d, hf).start()

    def kv_sibling(d, hf):
        there = kv.at[chip - d, core, hf]
        return remote(there, there, sbs.at[d, hf], sbr.at[d, hf], sibling)

    def make_rows(hf):
        sl = pl.ds(hf * HALF, HALF)
        cos, sin = cos_ref[sl, :], sin_ref[sl, :]

        def rotated(i):
            u = acc[sl, i * HEAD : (i + 1) * HEAD]
            u = u + (bq[i * HEAD : (i + 1) * HEAD] if i < HEADS else bk[...]).astype(F32)
            return (u * cos + pltpu.roll(u, HEAD // 2, 1) * sin).astype(BF16)

        kv[chip, core, hf, :, :HEAD] = rotated(HEADS)
        kv[chip, core, hf, :, HEAD:] = (
            acc[sl, (HEADS + 1) * HEAD :] + bv[...].astype(F32)
        ).astype(BF16)
        kv_start(hf, (0, 1), (0, 3), (1, 0), (3, 0), (0, 2))
        kv_sibling(0, hf).start()
        for h in range(HEADS):
            q = rotated(h)
            qn[h, sl, :] = q
            qt[:, pl.ds(h * ROWS + hf * HALF, HALF)] = q.T

    for u in range(4):
        issue(u)
    end0 = lengths[0]
    end1 = end0 + lengths[1]
    end2 = end1 + lengths[2]

    def start_at(index):
        later = jnp.where(index >= end2, end2, jnp.where(index >= end1, end1, end0))
        return jnp.where(index >= end0, later, 0)

    row_index = s * ROWS + lax.broadcasted_iota(jnp.int32, (1, ROWS), 1)
    first_key = start_at(row_index)
    index = s * ROWS + lax.broadcasted_iota(jnp.int32, (ROWS, HEAD), 0)
    angles = (index - start_at(index)).astype(F32) * freq_ref[...]
    cos_ref[...] = jnp.cos(angles)
    sine = jnp.sin(angles)
    lane = lax.broadcasted_iota(jnp.int32, (ROWS, HEAD), 1)
    sin_ref[...] = jnp.where(lane < HEAD // 2, -sine, sine)

    for copy in loads:
        copy.wait()
    acc[...] = nn(tok[...], w[t])
    pump(0)
    for copy in loads_out:
        copy.wait()
    gacc[...] = nt(grad[...], wo[t])
    m_s[...] = jnp.full(m_s.shape, neg_large, F32)
    l_s[...] = jnp.zeros(l_s.shape, F32)
    oacc[...] = jnp.zeros(oacc.shape, F32)
    pump(1)
    halves = [pl.ds(hf * HALF, HALF) for hf in range(2)]
    for hf, sl in enumerate(halves):
        if hf == 1:
            pump(2)
            pump(3)
            for u in range(4, 7):
                issue(u)
        acc[sl, :] += nn(tk[0, sl, :], w[left])
        acc[sl, :] += nn(tk[2, sl, :], w[right])
    for hf, sl in enumerate(halves):
        for u in (2 * hf, 2 * hf + 1):
            passed(u)
        acc[sl, :] += nn(tk[1, sl, :], w[opp])
        make_rows(hf)

    r2 = lax.broadcasted_iota(jnp.int32, (2 * HALF, ROWS), 0)
    key_at = jnp.where(r2 >= HALF, r2 + HALF, r2)

    def attend(first, second):
        both = jnp.concatenate(
            [
                kv[jnp.where(c < 0, chip, c), :, hf].reshape(2 * HALF, 2 * HEAD)
                for c, hf in (first, second)
            ],
            axis=0,
        )
        k = both[:, :HEAD]
        vt = both[:, HEAD:].T
        key = jnp.concatenate(
            [key_at + (c * (4 * HALF) + hf * HALF) for c, hf in (first, second)], axis=0
        )
        allowed = (key >= first_key) & (key <= row_index)
        following = nn(k, qt[:, :ROWS])
        held = None
        for h in range(HEADS + 1):
            sl = slice(h * ROWS, (h + 1) * ROWS)
            raw = following
            if h + 1 < HEADS:
                following = nn(k, qt[:, (h + 1) * ROWS : (h + 2) * ROWS])
            if held is not None:
                cols, weights, shrink = held
                oacc[:, cols] = oacc[:, cols] * shrink + nn(vt, weights)
            if h < HEADS:
                scores = jnp.where(allowed, raw * scale, neg_large)
                old = m_s[:, sl]
                top = jnp.maximum(old, jnp.max(scores, axis=0, keepdims=True))
                weights = jnp.exp2(scores - top)
                shrink = jnp.exp2(old - top)
                l_s[:, sl] = l_s[:, sl] * shrink + jnp.sum(weights, axis=0, keepdims=True)
                m_s[:, sl] = top
                held = (sl, weights.astype(BF16), shrink)

    def gather_grad(hf):
        sl = halves[hf]
        gacc[sl, :] += nt(gr[0, sl, :], wo[left])
        gacc[sl, :] += nt(gr[2, sl, :], wo[right])

    near = ((4, 1), (3, 8), (5, 2), (7, 6))

    def pick(j, e):
        values = [pair[e] for pair in near]
        return jnp.where(
            j == 0, values[0], jnp.where(j == 1, values[1], jnp.where(j == 2, values[2], values[3]))
        )

    def forward_step(i, carry):
        j, hf = lax.rem(i + 3, 4), lax.div(i + 3, 4) - 1
        is_own = i == 0
        ahead = (pick(j, 0), pick(j, 1))

        @pl.when(i == 1)
        def _():
            kv_third(0)
            kv_need(0, *near[0], *near[1])
            kv_second(1)
            pump(4)

        @pl.when(i == 2)
        def _():
            pump(5)

        @pl.when(i == 3)
        def _():
            kv_need(0, *near[2])
            gather_grad(0)

        @pl.when(i == 4)
        def _():
            kv_need(0, *near[3])
            kv_third(1)
            kv_need(1, *near[0], *near[1])
            pump(6)

        @pl.when(i == 5)
        def _():
            pump(7)

        @pl.when(i == 6)
        def _():
            kv_need(1, *near[2], *near[3])

        for d in ahead:
            @pl.when((i > 0) & (chip >= d))
            def _():
                kv_sibling(d, hf).wait_recv()

        @pl.when(is_own | (chip >= jnp.minimum(*ahead)))
        def _():
            attend(
                (jnp.where(is_own, chip, chip - ahead[0]), jnp.where(is_own, 0, hf)),
                (jnp.where(is_own, chip, chip - ahead[1]), jnp.where(is_own, 1, hf)),
            )

        return carry

    issue(7)
    kv_second(0)
    for hf in range(2):
        kv_sibling(0, hf).wait_recv()
    lax.fori_loop(0, REACH + 1, forward_step, 0)
    for h in range(HEADS):
        sl = slice(h * ROWS, (h + 1) * ROWS)
        mass = l_s[:, sl]
        o = (oacc[:, sl] / mass).astype(BF16)
        att[:, sl] = o
        at[:, h * HEAD : (h + 1) * HEAD] = o.T
        lse[:, sl] = m_s[:, sl] + jnp.log2(mass)

    def pieces(n):
        return ((0, HALF), (HALF, HALF)) if n == 0 else (
            ((n - 1) * HALF, CHUNK), ((n - 1) * HALF + CHUNK, CHUNK)
        )

    def passing_rows(n):
        return pl.ds(0, HALF) if n == 0 else pl.ds((n - 1) * CHUNK, CHUNK)

    def scatter_copy(i, part, arrived, passing, n):
        a, b = [pl.ds(*piece) for piece in pieces(n)]
        over = passing_rows(n)
        src, dst, device = (
            (part.at[1, a], passing.at[0, over], to_right),
            (part.at[1, b], passing.at[1, over], to_left),
            (part.at[2, b], arrived.at[0, b], to_right),
            (part.at[0, a], arrived.at[1, a], to_left),
            (part.at[2, a], arrived.at[0, a], to_right),
            (part.at[0, b], arrived.at[1, b], to_left),
        )[i]
        return remote(src, dst, rss.at[n, i], rsr.at[n, i], device)

    def scatter_early(share, part, arrived, passing, n):
        (first, rows), (second, _) = pieces(n)
        both = pl.ds(first, 2 * rows)
        part[1, both, :] = share(opp, both).astype(BF16)
        for i in range(2):
            scatter_copy(i, part, arrived, passing, n).start()
        mine = share(right, both)
        part[2, pl.ds(second, rows), :] = mine[rows:].astype(BF16)
        scatter_copy(2, part, arrived, passing, n).start()
        kept[0, pl.ds(0, rows), :] = mine[:rows]
        mine = share(left, both)
        part[0, pl.ds(first, rows), :] = mine[:rows].astype(BF16)
        scatter_copy(3, part, arrived, passing, n).start()
        kept[1, pl.ds(0, rows), :] = mine[rows:]

    def scatter_late(part, arrived, passing, n):
        for i, rel in ((0, 2), (1, 0)):
            base, rows = pieces(n)[i]
            scatter_copy(i, part, arrived, passing, n).wait_recv()
            part[rel, pl.ds(base, rows), :] = (
                kept[i, pl.ds(0, rows), :] + passing[i, passing_rows(n), :].astype(F32)
            ).astype(BF16)
            scatter_copy(4 + i, part, arrived, passing, n).start()

    def scatter_end(share, part, arrived, passing, n, result):
        (first, rows), _ = pieces(n)
        both = pl.ds(first, 2 * rows)
        mine = share(t, both)
        for i in range(2, 6):
            scatter_copy(i, part, arrived, passing, n).wait_recv()
        result[both, :] = (
            mine + arrived[0, both, :].astype(F32) + arrived[1, both, :].astype(F32)
        ).astype(BF16)
        for i in range(6):
            scatter_copy(i, part, arrived, passing, n).wait_send()

    def out_share(slot, sl):
        return nn(at[sl, :], wo[slot])

    scatter_early(out_share, p_out, v_out, f_out, 0)

    gather_grad(1)
    for hf in range(2):
        sl = pl.ds(hf * HALF, HALF)
        for u in (4 + 2 * hf, 5 + 2 * hf):
            passed(u)
        g = (gacc[sl, :] + nt(gr[1, sl, :], wo[opp])).astype(BF16)
        for h in range(HEADS):
            part = g[:, h * HEAD : (h + 1) * HEAD]
            gn[h, sl, :] = part
            gt[:, pl.ds(h * ROWS + hf * HALF, HALF)] = part.T
    delta[...] = jnp.sum(gt[...].astype(F32) * att[...].astype(F32), axis=0, keepdims=True)
    oacc[...] = jnp.zeros(oacc.shape, F32)

    def dkv_sibling(d, hf):
        return remote(sib_out.at[d, hf], sib_in.at[d, hf], dss.at[d, hf], dsr.at[d, hf], sibling)

    def dkv_send(d, hf):
        return remote(
            dkv_out.at[d - 1, hf], dkv_in.at[d - 1, hf], dos.at[d - 1, hf], dor.at[d - 1, hf],
            {"seq": s - 2 * d, "tp": t},
        )

    def backward(d, hf):
        both = kv[chip - d, :, hf].reshape(2 * HALF, 2 * HEAD)
        k, v = both[:, :HEAD], both[:, HEAD:]
        kt = k.T
        key = key_at + ((chip - d) * (4 * HALF) + hf * HALF)
        allowed = (key >= first_key) & (key <= row_index)
        following = (nn(k, qt[:, :ROWS]), nn(v, gt[:, :ROWS]))
        held = None
        dk = jnp.zeros((2 * HALF, HEAD), F32)
        dv = jnp.zeros((2 * HALF, HEAD), F32)
        for h in range(HEADS + 1):
            sl = slice(h * ROWS, (h + 1) * ROWS)
            raw, dprob = following
            if h + 1 < HEADS:
                nxt = slice((h + 1) * ROWS, (h + 2) * ROWS)
                following = (nn(k, qt[:, nxt]), nn(v, gt[:, nxt]))
            if held is not None:
                cols, prob_b, ds_b = held
                dv = dv + nn(prob_b, gn[h - 1])
                dk = dk + nn(ds_b, qn[h - 1])
                oacc[:, cols] = oacc[:, cols] + nn(kt, ds_b)
            if h < HEADS:
                prob = jnp.where(allowed, jnp.exp2(raw * scale - lse[:, sl]), 0.0)
                ds = prob * (dprob - delta[:, sl])
                held = (sl, prob.astype(BF16), ds.astype(BF16))
        tmp[:, :, :HEAD] = (dk * factor).reshape(2, HALF, HEAD)
        tmp[:, :, HEAD:] = dv.reshape(2, HALF, HEAD)
        own[d, hf] = tmp[core]
        sib_out[d, hf] = tmp[1 - core].astype(BF16)
        dkv_sibling(d, hf).start()

    span = REACH + 1

    def dkv_pump(i):
        d, hf = REACH - lax.rem(i, span), lax.div(i, span)

        @pl.when((chip >= d) & (d > 0))
        def _():
            dkv_sibling(d, hf).wait_recv()
            dkv_out[d - 1, hf] = (own[d, hf] + sib_in[d, hf].astype(F32)).astype(BF16)
            dkv_send(d, hf).start()

    def backward_step(i, carry):
        d, hf = REACH - lax.rem(i, span), lax.div(i, span)

        @pl.when(chip >= d)
        def _():
            backward(d, hf)

        @pl.when(i > 0)
        def _():
            dkv_pump(i - 1)

        @pl.when(i == span - 1)
        def _():
            scatter_late(p_out, v_out, f_out, 0)

        return carry

    lax.fori_loop(0, 2 * span, backward_step, 0)
    for h in range(HEADS):
        u = oacc[:, h * ROWS : (h + 1) * ROWS].T * factor
        x[:, h * HEAD : (h + 1) * HEAD] = (
            u * cos_ref[...] - pltpu.roll(u, HEAD // 2, 1) * sin_ref[...]
        ).astype(BF16)
    def finish_pair(hf):
        dkv_sibling(0, hf).wait_recv()
        own[0, hf] = own[0, hf] + sib_in[0, hf].astype(F32)
        for d in range(1, REACH + 1):
            @pl.when(chip + d < CHIPS)
            def _():
                dkv_send(d, hf).wait_recv()
                own[0, hf] = own[0, hf] + dkv_in[d - 1, hf].astype(F32)
        sl = pl.ds(hf * HALF, HALF)
        u = own[0, hf, :, :HEAD]
        x[sl, FEAT : FEAT + HEAD] = (
            u * cos_ref[sl, :] - pltpu.roll(u, HEAD // 2, 1) * sin_ref[sl, :]
        ).astype(BF16)
        x[sl, FEAT + HEAD :] = own[0, hf, :, HEAD:].astype(BF16)

    def grad_share(slot, sl):
        return nt(x[sl, :], w[slot])

    finish_pair(0)
    scatter_early(grad_share, p_grad, v_grad, f_grad, 1)
    scatter_end(out_share, p_out, v_out, f_out, 0, out_ref)
    scatter_late(p_grad, v_grad, f_grad, 1)
    finish_pair(1)
    scatter_early(grad_share, p_grad, v_grad, f_grad, 2)
    scatter_end(grad_share, p_grad, v_grad, f_grad, 1, gtok_ref)
    scatter_late(p_grad, v_grad, f_grad, 2)

    for u in range(8):
        for way in range(2):
            send(u, way).wait_send()
            forward(u, way).wait_send()
    for hf in range(2):
        for j in range(1, 16):
            slot = (j // 4, j % 4)
            kv_copy(hf, *slot).wait_send()
            if slot not in relayed:
                gap = chip - place(*slot)

                @pl.when((gap < 1) | (gap > REACH))
                def _():
                    kv_wait(hf, slot)
        for d in range(REACH + 1):
            @pl.when(chip >= d)
            def _():
                kv_sibling(d, hf).wait_send()
                dkv_sibling(d, hf).wait_send()
                if d > 0:
                    dkv_send(d, hf).wait_send()
    scatter_end(grad_share, p_grad, v_grad, f_grad, 2, gtok_ref)


def hand_over(a, b, c, d):
    c[...] = a[...]
    d[...] = b[...]


def local(
    tokens, w_query, b_query, w_key, key_bias, value_weight, value_bias, w_out, doc_lengths, grad_out
):
    freq = theta_base ** (-2.0 * np.arange(HEAD // 2) / HEAD)
    freq = jnp.asarray(np.concatenate([freq, freq])[None, :], F32)
    vm = pl.BlockSpec(memory_space=pltpu.VMEM)
    hbm = pl.BlockSpec(memory_space=pl.ANY)
    dma = pltpu.SemaphoreType.DMA
    shape = jax.ShapeDtypeStruct((ROWS, WIDTH), BF16)
    results = pl.pallas_call(
        block_kernel,
        out_shape=(shape, shape),
        in_specs=[pl.BlockSpec(memory_space=pltpu.SMEM), vm, vm, hbm, hbm, hbm, hbm, vm, vm, vm, vm],
        out_specs=(vm, vm),
        scratch_shapes=[
            pltpu.VMEM((ROWS, HEAD), F32),
            pltpu.VMEM((ROWS, HEAD), F32),
            pltpu.VMEM((4, WIDTH, FEAT + 2 * HEAD), BF16),
            pltpu.VMEM((4, FEAT, WIDTH), BF16),
            pltpu.VMEM((3, ROWS, WIDTH), BF16),
            pltpu.VMEM((3, ROWS, WIDTH), BF16),
            pltpu.VMEM((ROWS, FEAT + 2 * HEAD), F32),
            pltpu.VMEM((ROWS, FEAT), F32),
            pltpu.VMEM((HEADS, ROWS, HEAD), BF16),
            pltpu.VMEM((HEAD, HEADS * ROWS), BF16),
            pltpu.VMEM((HEADS, ROWS, HEAD), BF16),
            pltpu.VMEM((HEAD, HEADS * ROWS), BF16),
            pltpu.VMEM((CHIPS, 2, 2, HALF, 2 * HEAD), BF16),
            pltpu.VMEM((ROWS, FEAT), BF16),
            pltpu.VMEM((HEAD, HEADS * ROWS), BF16),
            pltpu.VMEM((HEAD, HEADS * ROWS), F32),
            pltpu.VMEM((1, HEADS * ROWS), F32),
            pltpu.VMEM((1, HEADS * ROWS), F32),
            pltpu.VMEM((1, HEADS * ROWS), F32),
            pltpu.VMEM((1, HEADS * ROWS), F32),
            pltpu.VMEM((2, HALF, 2 * HEAD), F32),
            pltpu.VMEM((REACH + 1, 2, HALF, 2 * HEAD), F32),
            pltpu.VMEM((REACH + 1, 2, HALF, 2 * HEAD), BF16),
            pltpu.VMEM((REACH + 1, 2, HALF, 2 * HEAD), BF16),
            pltpu.VMEM((REACH, 2, HALF, 2 * HEAD), BF16),
            pltpu.VMEM((REACH, 2, HALF, 2 * HEAD), BF16),
            pltpu.VMEM((ROWS, FEAT + 2 * HEAD), BF16),
            pltpu.VMEM((3, ROWS, WIDTH), BF16),
            pltpu.VMEM((2, ROWS, WIDTH), BF16),
            pltpu.VMEM((2, HALF, WIDTH), BF16),
            pltpu.VMEM((3, ROWS, WIDTH), BF16),
            pltpu.VMEM((2, ROWS, WIDTH), BF16),
            pltpu.VMEM((2, HALF, WIDTH), BF16),
            pltpu.VMEM((2, HALF, WIDTH), F32),
            dma((16,)),
            dma((8, 2)), dma((8, 2)),
            dma((8, 2)), dma((8, 2)),
            dma((2, 4, 4)), dma((2, 4, 4)),
            dma((REACH + 1, 2)), dma((REACH + 1, 2)),
            dma((REACH + 1, 2)), dma((REACH + 1, 2)),
            dma((REACH, 2)), dma((REACH, 2)),
            dma((3, 6)), dma((3, 6)),
        ],
        compiler_params=pltpu.CompilerParams(
            collective_id=0, has_side_effects=True, vmem_limit_bytes=60 << 20
        ),
        name="attention_block",
    )(
        doc_lengths, tokens, grad_out, w_query, w_key, value_weight, w_out,
        b_query, key_bias, value_bias, freq,
    )
    return pl.pallas_call(
        hand_over,
        out_shape=(shape, shape),
        in_specs=[vm, vm],
        out_specs=(vm, vm),
        name="hand_over",
    )(*results)


def solution(mesh):
    return jax.shard_map(
        local,
        mesh=mesh,
        in_specs=(
            P("seq", "tp"),
            P(None, "tp"),
            P("tp"),
            P(None, "tp"),
            P("tp"),
            P(None, "tp"),
            P("tp"),
            P("tp", None),
            P(),
            P("seq", "tp"),
        ),
        out_specs=(P("seq", "tp"), P("seq", "tp")),
        check_vma=False,
    )
```

```python
import functools

import jax
import jax.numpy as jnp
import numpy as np
from jax import lax
from jax.experimental import pallas as pl
from jax.experimental.pallas import tpu as pltpu
from jax.sharding import PartitionSpec as P

theta_base = 1000000.0
neg_large = -1e30
log2e = 1.4426950408889634
HEAD = 128
ROWS = 256
HALF = 128
CHUNK = 64
HEADS = 5
WIDTH = 1280
FEAT = HEADS * HEAD
CHIPS = 16
REACH = 8
F32 = jnp.float32
BF16 = jnp.bfloat16
MESH = pl.DeviceIdType.MESH
factor = HEAD**-0.5
scale = factor * log2e


def nn(a, b):
    return lax.dot_general(a, b, (((1,), (0,)), ((), ())), preferred_element_type=F32)


def nt(a, b):
    return lax.dot_general(a, b, (((1,), (1,)), ((), ())), preferred_element_type=F32)


def block_kernel(
    lengths, tok, grad, wq_hbm, wk_hbm, wv_hbm, wo_hbm, bq, bk, bv, freq_ref,
    out_ref, gtok_ref,
    cos_ref, sin_ref, w, wo, tk, gr, acc, gacc, qn, qt, gn, gt, kv, at, att, oacc, m_s, l_s, lse, delta,
    tmp, own, sib_out, sib_in, dkv_out, dkv_in, x, p_out, v_out, f_out, p_grad, v_grad, f_grad, kept,
    wsem, ys, yr, fs, fr, kvs, kvr, sbs, sbr, dss, dsr, dos, dor, rss, rsr,
):
    s = lax.axis_index("seq")
    t = lax.axis_index("tp")
    chip, core = lax.div(s, 2), lax.rem(s, 2)
    right, left, opp = lax.rem(t + 1, 4), lax.rem(t + 3, 4), lax.rem(t + 2, 4)
    to_right, to_left = {"seq": s, "tp": right}, {"seq": s, "tp": left}
    sibling = {"seq": s + 1 - 2 * core, "tp": t}
    at_z, at_x = lax.div(chip, 4), lax.rem(chip, 4)
    m1 = at_x + core * (at_z - at_x)
    m2 = at_z + core * (at_x - at_z)
    stride1, stride2 = 1 + 3 * core, 4 - 3 * core

    def place(r2, r1):
        return lax.rem(m1 + 4 - r1, 4) * stride1 + lax.rem(m2 + 4 - r2, 4) * stride2

    def towards(step2, step1):
        return {"seq": 2 * place(-step2, -step1) + core, "tp": t}

    up1, down1, up2, down2 = towards(0, 1), towards(0, -1), towards(1, 0), towards(-1, 0)
    across1 = towards(0, 2)

    def remote(src, dst, send, recv, device):
        return pltpu.make_async_remote_copy(
            src_ref=src, dst_ref=dst, send_sem=send, recv_sem=recv,
            device_id=device, device_id_type=MESH,
        )

    loads = []
    for i in range(4):
        for j, (ref, lo, hi) in enumerate(
            ((wq_hbm, 0, FEAT), (wk_hbm, FEAT, FEAT + HEAD), (wv_hbm, FEAT + HEAD, FEAT + 2 * HEAD))
        ):
            loads.append(
                pltpu.make_async_copy(
                    ref.at[pl.ds(i * WIDTH, WIDTH)], w.at[i, :, lo:hi], wsem.at[3 * i + j]
                )
            )
    loads_out = [
        pltpu.make_async_copy(wo_hbm.at[:, pl.ds(i * WIDTH, WIDTH)], wo.at[i], wsem.at[12 + i])
        for i in range(4)
    ]
    for copy in loads + loads_out:
        copy.start()

    barrier = pltpu.get_barrier_semaphore()
    partners = (to_right, to_left, sibling, up1, down1, up2, down2, across1)
    for device in partners:
        pl.semaphore_signal(barrier, inc=1, device_id=device, device_id_type=MESH)
    for d in range(1, REACH + 1):
        @pl.when(chip + d < CHIPS)
        def _():
            pl.semaphore_signal(
                barrier, inc=1, device_id={"seq": s + 2 * d, "tp": t}, device_id_type=MESH
            )

        @pl.when(chip >= d)
        def _():
            pl.semaphore_signal(
                barrier, inc=1, device_id={"seq": s - 2 * d, "tp": t}, device_id_type=MESH
            )
    pl.semaphore_wait(
        barrier,
        len(partners) + jnp.minimum(chip, REACH) + jnp.minimum(CHIPS - 1 - chip, REACH),
    )

    def unit(u):
        src, buf = (tok, tk) if u < 4 else (grad, gr)
        return src, buf, pl.ds((u % 4) * CHUNK, CHUNK)

    def send(u, way):
        src, buf, sl = unit(u)
        if way == 0:
            return remote(src.at[sl], buf.at[0, sl], ys.at[u, 0], yr.at[u, 0], to_right)
        return remote(src.at[sl], buf.at[2, sl], ys.at[u, 1], yr.at[u, 1], to_left)

    def forward(u, way):
        _, buf, _ = unit(u)
        sl = pl.ds((u % 4) * CHUNK + way * (CHUNK // 2), CHUNK // 2)
        return remote(
            buf.at[2 * way, sl], buf.at[1, sl], fs.at[u, way], fr.at[u, way],
            to_left if way else to_right,
        )

    def issue(u):
        for way in range(2):
            send(u, way).start()

    def pump(u):
        for way in range(2):
            send(u, way).wait_recv()
            forward(u, way).start()

    def passed(u):
        for way in range(2):
            forward(u, way).wait_recv()

    def kv_copy(hf, r2, r1):
        if r2 == 0:
            src = (0, 0)
            device = (up1, across1, down1)[r1 - 1]
        elif r2 == 2:
            src, device = ((1, r1), up2) if r1 < 2 else ((3, r1), down2)
        else:
            src, device = (0, r1), up2 if r2 == 1 else down2
        here = kv.at[place(*src), core, hf]
        return remote(here, here, kvs.at[hf, r2, r1], kvr.at[hf, r2, r1], device)

    def kv_start(hf, *slots):
        for slot in slots:
            kv_copy(hf, *slot).start()

    def kv_wait(hf, *slots):
        for r2, r1 in slots:
            there = kv.at[place(r2, r1), core, hf]
            remote(there, there, kvs.at[hf, r2, r1], kvr.at[hf, r2, r1], sibling).wait_recv()

    def kv_second(hf):
        kv_wait(hf, (1, 0))
        kv_start(hf, (2, 0))
        for r1 in (1, 3, 2):
            kv_wait(hf, (0, r1))
            kv_start(hf, (1, r1), (3, r1))

    def kv_third(hf):
        kv_wait(hf, (1, 1))
        kv_start(hf, (2, 1))
        kv_wait(hf, (3, 3))
        kv_start(hf, (2, 3))
        kv_wait(hf, (3, 2))
        kv_start(hf, (2, 2))

    relayed = ((0, 1), (0, 2), (0, 3), (1, 0), (1, 1), (3, 2), (3, 3))

    def kv_need(hf, *distances):
        for d in distances:
            @pl.when(chip >= d)
            def _():
                back_z = at_z - lax.div(chip - d, 4)
                back_x = lax.rem(at_x + 4 - lax.rem(chip - d, 4), 4)
                r1 = back_x + core * (back_z - back_x)
                r2 = back_z + core * (back_x - back_z)
                waited = (r2 == 0) | ((r2 == 1) & (r1 < 2)) | ((r2 == 3) & (r1 >= 2))

                @pl.when(jnp.logical_not(waited))
                def _():
                    kv_wait(hf, (r2, r1))

                kv_sibling(d, hf).start()

    def kv_sibling(d, hf):
        there = kv.at[chip - d, core, hf]
        return remote(there, there, sbs.at[d, hf], sbr.at[d, hf], sibling)

    def make_rows(hf):
        sl = pl.ds(hf * HALF, HALF)
        cos, sin = cos_ref[sl, :], sin_ref[sl, :]

        def rotated(i):
            u = acc[sl, i * HEAD : (i + 1) * HEAD]
            u = u + (bq[i * HEAD : (i + 1) * HEAD] if i < HEADS else bk[...]).astype(F32)
            return (u * cos + pltpu.roll(u, HEAD // 2, 1) * sin).astype(BF16)

        kv[chip, core, hf, :, :HEAD] = rotated(HEADS)
        kv[chip, core, hf, :, HEAD:] = (
            acc[sl, (HEADS + 1) * HEAD :] + bv[...].astype(F32)
        ).astype(BF16)
        kv_start(hf, (0, 1), (0, 3), (1, 0), (3, 0), (0, 2))
        kv_sibling(0, hf).start()
        for h in range(HEADS):
            q = rotated(h)
            qn[h, sl, :] = q
            qt[:, pl.ds(h * ROWS + hf * HALF, HALF)] = q.T

    for u in range(4):
        issue(u)
    end0 = lengths[0]
    end1 = end0 + lengths[1]
    end2 = end1 + lengths[2]

    def start_at(index):
        later = jnp.where(index >= end2, end2, jnp.where(index >= end1, end1, end0))
        return jnp.where(index >= end0, later, 0)

    row_index = s * ROWS + lax.broadcasted_iota(jnp.int32, (1, ROWS), 1)
    first_key = start_at(row_index)
    index = s * ROWS + lax.broadcasted_iota(jnp.int32, (ROWS, HEAD), 0)
    angles = (index - start_at(index)).astype(F32) * freq_ref[...]
    cos_ref[...] = jnp.cos(angles)
    sine = jnp.sin(angles)
    lane = lax.broadcasted_iota(jnp.int32, (ROWS, HEAD), 1)
    sin_ref[...] = jnp.where(lane < HEAD // 2, -sine, sine)

    for copy in loads:
        copy.wait()
    acc[...] = nn(tok[...], w[t])
    pump(0)
    for copy in loads_out:
        copy.wait()
    gacc[...] = nt(grad[...], wo[t])
    m_s[...] = jnp.full(m_s.shape, neg_large, F32)
    l_s[...] = jnp.zeros(l_s.shape, F32)
    oacc[...] = jnp.zeros(oacc.shape, F32)
    pump(1)
    halves = [pl.ds(hf * HALF, HALF) for hf in range(2)]
    for hf, sl in enumerate(halves):
        if hf == 1:
            pump(2)
            pump(3)
            for u in range(4, 7):
                issue(u)
        acc[sl, :] += nn(tk[0, sl, :], w[left])
        acc[sl, :] += nn(tk[2, sl, :], w[right])
    for hf, sl in enumerate(halves):
        for u in (2 * hf, 2 * hf + 1):
            passed(u)
        acc[sl, :] += nn(tk[1, sl, :], w[opp])
        make_rows(hf)

    r2 = lax.broadcasted_iota(jnp.int32, (2 * HALF, ROWS), 0)
    key_at = jnp.where(r2 >= HALF, r2 + HALF, r2)

    def attend(first, second):
        both = jnp.concatenate(
            [
                kv[jnp.where(c < 0, chip, c), :, hf].reshape(2 * HALF, 2 * HEAD)
                for c, hf in (first, second)
            ],
            axis=0,
        )
        k = both[:, :HEAD]
        vt = both[:, HEAD:].T
        key = jnp.concatenate(
            [key_at + (c * (4 * HALF) + hf * HALF) for c, hf in (first, second)], axis=0
        )
        allowed = (key >= first_key) & (key <= row_index)
        following = nn(k, qt[:, :ROWS])
        held = None
        for h in range(HEADS + 1):
            sl = slice(h * ROWS, (h + 1) * ROWS)
            raw = following
            if h + 1 < HEADS:
                following = nn(k, qt[:, (h + 1) * ROWS : (h + 2) * ROWS])
            if held is not None:
                cols, weights, shrink = held
                oacc[:, cols] = oacc[:, cols] * shrink + nn(vt, weights)
            if h < HEADS:
                scores = jnp.where(allowed, raw * scale, neg_large)
                old = m_s[:, sl]
                top = jnp.maximum(old, jnp.max(scores, axis=0, keepdims=True))
                weights = jnp.exp2(scores - top)
                shrink = jnp.exp2(old - top)
                l_s[:, sl] = l_s[:, sl] * shrink + jnp.sum(weights, axis=0, keepdims=True)
                m_s[:, sl] = top
                held = (sl, weights.astype(BF16), shrink)

    near = ((4, 1), (3, 8), (5, 2), (7, 6))

    def pick(j, e):
        values = [pair[e] for pair in near]
        return jnp.where(
            j == 0, values[0], jnp.where(j == 1, values[1], jnp.where(j == 2, values[2], values[3]))
        )

    def forward_step(i, carry):
        j, hf = lax.rem(i + 3, 4), lax.div(i + 3, 4) - 1
        is_own = i == 0
        ahead = (pick(j, 0), pick(j, 1))

        @pl.when(i == 1)
        def _():
            kv_third(0)
            kv_need(0, *near[0], *near[1])
            kv_second(1)
            pump(4)

        @pl.when(i == 2)
        def _():
            pump(5)

        @pl.when(i == 3)
        def _():
            kv_need(0, *near[2], *near[3])

        @pl.when(i == 4)
        def _():
            kv_third(1)
            kv_need(1, *near[0], *near[1])
            pump(6)

        @pl.when(i == 5)
        def _():
            pump(7)

        @pl.when(i == 6)
        def _():
            kv_need(1, *near[2], *near[3])

        for d in ahead:
            @pl.when((i > 0) & (chip >= d))
            def _():
                kv_sibling(d, hf).wait_recv()

        @pl.when(is_own | (chip >= jnp.minimum(*ahead)))
        def _():
            attend(
                (jnp.where(is_own, chip, chip - ahead[0]), jnp.where(is_own, 0, hf)),
                (jnp.where(is_own, chip, chip - ahead[1]), jnp.where(is_own, 1, hf)),
            )

        return carry

    issue(7)
    kv_second(0)
    for hf in range(2):
        kv_sibling(0, hf).wait_recv()
    lax.fori_loop(0, REACH + 1, forward_step, 0)
    for h in range(HEADS):
        sl = slice(h * ROWS, (h + 1) * ROWS)
        mass = l_s[:, sl]
        o = (oacc[:, sl] / mass).astype(BF16)
        att[:, sl] = o
        at[:, h * HEAD : (h + 1) * HEAD] = o.T
        lse[:, sl] = m_s[:, sl] + jnp.log2(mass)

    def pieces(n):
        return ((0, HALF), (HALF, HALF)) if n == 0 else (
            ((n - 1) * HALF, CHUNK), ((n - 1) * HALF + CHUNK, CHUNK)
        )

    def passing_rows(n):
        return pl.ds(0, HALF) if n == 0 else pl.ds((n - 1) * CHUNK, CHUNK)

    def scatter_copy(i, part, arrived, passing, n):
        a, b = [pl.ds(*piece) for piece in pieces(n)]
        over = passing_rows(n)
        src, dst, device = (
            (part.at[1, a], passing.at[0, over], to_right),
            (part.at[1, b], passing.at[1, over], to_left),
            (part.at[2, b], arrived.at[0, b], to_right),
            (part.at[0, a], arrived.at[1, a], to_left),
            (part.at[2, a], arrived.at[0, a], to_right),
            (part.at[0, b], arrived.at[1, b], to_left),
        )[i]
        return remote(src, dst, rss.at[n, i], rsr.at[n, i], device)

    def scatter_early(share, part, arrived, passing, n):
        (first, rows), (second, _) = pieces(n)
        both = pl.ds(first, 2 * rows)
        part[1, both, :] = share(opp, both).astype(BF16)
        for i in range(2):
            scatter_copy(i, part, arrived, passing, n).start()
        mine = share(right, both)
        part[2, pl.ds(second, rows), :] = mine[rows:].astype(BF16)
        scatter_copy(2, part, arrived, passing, n).start()
        kept[0, pl.ds(0, rows), :] = mine[:rows]
        mine = share(left, both)
        part[0, pl.ds(first, rows), :] = mine[:rows].astype(BF16)
        scatter_copy(3, part, arrived, passing, n).start()
        kept[1, pl.ds(0, rows), :] = mine[rows:]

    def scatter_late(part, arrived, passing, n):
        for i, rel in ((0, 2), (1, 0)):
            base, rows = pieces(n)[i]
            scatter_copy(i, part, arrived, passing, n).wait_recv()
            part[rel, pl.ds(base, rows), :] = (
                kept[i, pl.ds(0, rows), :] + passing[i, passing_rows(n), :].astype(F32)
            ).astype(BF16)
            scatter_copy(4 + i, part, arrived, passing, n).start()

    def scatter_end(share, part, arrived, passing, n, result):
        (first, rows), _ = pieces(n)
        both = pl.ds(first, 2 * rows)
        mine = share(t, both)
        for i in range(2, 6):
            scatter_copy(i, part, arrived, passing, n).wait_recv()
        result[both, :] = (
            mine + arrived[0, both, :].astype(F32) + arrived[1, both, :].astype(F32)
        ).astype(BF16)
        for i in range(6):
            scatter_copy(i, part, arrived, passing, n).wait_send()

    def out_share(slot, sl):
        return nn(at[sl, :], wo[slot])

    scatter_early(out_share, p_out, v_out, f_out, 0)

    for u in range(4, 8):
        passed(u)
    g = gacc[...] + nt(gr[0], wo[left])
    g = g + nt(gr[2], wo[right])
    g = (g + nt(gr[1], wo[opp])).astype(BF16)
    for h in range(HEADS):
        part = g[:, h * HEAD : (h + 1) * HEAD]
        gn[h] = part
        gt[:, h * ROWS : (h + 1) * ROWS] = part.T
    delta[...] = jnp.sum(gt[...].astype(F32) * att[...].astype(F32), axis=0, keepdims=True)
    oacc[...] = jnp.zeros(oacc.shape, F32)

    def dkv_sibling(d, hf):
        return remote(sib_out.at[d, hf], sib_in.at[d, hf], dss.at[d, hf], dsr.at[d, hf], sibling)

    def dkv_send(d, hf):
        return remote(
            dkv_out.at[d - 1, hf], dkv_in.at[d - 1, hf], dos.at[d - 1, hf], dor.at[d - 1, hf],
            {"seq": s - 2 * d, "tp": t},
        )

    def backward(d, hf):
        both = kv[chip - d, :, hf].reshape(2 * HALF, 2 * HEAD)
        k, v = both[:, :HEAD], both[:, HEAD:]
        kt = k.T
        key = key_at + ((chip - d) * (4 * HALF) + hf * HALF)
        allowed = (key >= first_key) & (key <= row_index)
        following = (nn(k, qt[:, :ROWS]), nn(v, gt[:, :ROWS]))
        held = None
        dk = jnp.zeros((2 * HALF, HEAD), F32)
        dv = jnp.zeros((2 * HALF, HEAD), F32)
        for h in range(HEADS + 1):
            sl = slice(h * ROWS, (h + 1) * ROWS)
            raw, dprob = following
            if h + 1 < HEADS:
                nxt = slice((h + 1) * ROWS, (h + 2) * ROWS)
                following = (nn(k, qt[:, nxt]), nn(v, gt[:, nxt]))
            if held is not None:
                cols, prob_b, ds_b = held
                dv = dv + nn(prob_b, gn[h - 1])
                dk = dk + nn(ds_b, qn[h - 1])
                oacc[:, cols] = oacc[:, cols] + nn(kt, ds_b)
            if h < HEADS:
                prob = jnp.where(allowed, jnp.exp2(raw * scale - lse[:, sl]), 0.0)
                ds = prob * (dprob - delta[:, sl])
                held = (sl, prob.astype(BF16), ds.astype(BF16))
        tmp[:, :, :HEAD] = (dk * factor).reshape(2, HALF, HEAD)
        tmp[:, :, HEAD:] = dv.reshape(2, HALF, HEAD)
        own[d, hf] = tmp[core]
        sib_out[d, hf] = tmp[1 - core].astype(BF16)
        dkv_sibling(d, hf).start()

    span = REACH + 1

    def dkv_pump(i):
        d, hf = REACH - lax.rem(i, span), lax.div(i, span)

        @pl.when((chip >= d) & (d > 0))
        def _():
            dkv_sibling(d, hf).wait_recv()
            dkv_out[d - 1, hf] = (own[d, hf] + sib_in[d, hf].astype(F32)).astype(BF16)
            dkv_send(d, hf).start()

    def backward_step(i, carry):
        d, hf = REACH - lax.rem(i, span), lax.div(i, span)

        @pl.when(chip >= d)
        def _():
            backward(d, hf)

        @pl.when(i > 0)
        def _():
            dkv_pump(i - 1)

        @pl.when(i == span - 2)
        def _():
            scatter_late(p_out, v_out, f_out, 0)

        return carry

    lax.fori_loop(0, 2 * span, backward_step, 0)
    def query_rows(hf):
        sl = halves[hf]
        for h in range(HEADS):
            u = oacc[:, pl.ds(h * ROWS + hf * HALF, HALF)].T * factor
            x[sl, h * HEAD : (h + 1) * HEAD] = (
                u * cos_ref[sl, :] - pltpu.roll(u, HEAD // 2, 1) * sin_ref[sl, :]
            ).astype(BF16)

    def finish_pair(hf):
        dkv_sibling(0, hf).wait_recv()
        own[0, hf] = own[0, hf] + sib_in[0, hf].astype(F32)
        for d in range(1, REACH + 1):
            @pl.when(chip + d < CHIPS)
            def _():
                dkv_send(d, hf).wait_recv()
                own[0, hf] = own[0, hf] + dkv_in[d - 1, hf].astype(F32)
        sl = pl.ds(hf * HALF, HALF)
        u = own[0, hf, :, :HEAD]
        x[sl, FEAT : FEAT + HEAD] = (
            u * cos_ref[sl, :] - pltpu.roll(u, HEAD // 2, 1) * sin_ref[sl, :]
        ).astype(BF16)
        x[sl, FEAT + HEAD :] = own[0, hf, :, HEAD:].astype(BF16)

    def grad_share(slot, sl):
        return nt(x[sl, :], w[slot])

    query_rows(0)
    finish_pair(0)
    scatter_early(grad_share, p_grad, v_grad, f_grad, 1)
    query_rows(1)
    scatter_end(out_share, p_out, v_out, f_out, 0, out_ref)
    scatter_late(p_grad, v_grad, f_grad, 1)
    finish_pair(1)
    scatter_early(grad_share, p_grad, v_grad, f_grad, 2)
    scatter_end(grad_share, p_grad, v_grad, f_grad, 1, gtok_ref)
    scatter_late(p_grad, v_grad, f_grad, 2)

    for u in range(8):
        for way in range(2):
            send(u, way).wait_send()
            forward(u, way).wait_send()
    for hf in range(2):
        for j in range(1, 16):
            slot = (j // 4, j % 4)
            kv_copy(hf, *slot).wait_send()
            if slot not in relayed:
                gap = chip - place(*slot)

                @pl.when((gap < 1) | (gap > REACH))
                def _():
                    kv_wait(hf, slot)
        for d in range(REACH + 1):
            @pl.when(chip >= d)
            def _():
                kv_sibling(d, hf).wait_send()
                dkv_sibling(d, hf).wait_send()
                if d > 0:
                    dkv_send(d, hf).wait_send()
    scatter_end(grad_share, p_grad, v_grad, f_grad, 2, gtok_ref)


def hand_over(a, b, c, d):
    c[...] = a[...]
    d[...] = b[...]


def local(
    tokens, w_query, b_query, w_key, key_bias, value_weight, value_bias, w_out, doc_lengths, grad_out
):
    freq = theta_base ** (-2.0 * np.arange(HEAD // 2) / HEAD)
    freq = jnp.asarray(np.concatenate([freq, freq])[None, :], F32)
    vm = pl.BlockSpec(memory_space=pltpu.VMEM)
    hbm = pl.BlockSpec(memory_space=pl.ANY)
    dma = pltpu.SemaphoreType.DMA
    shape = jax.ShapeDtypeStruct((ROWS, WIDTH), BF16)
    results = pl.pallas_call(
        block_kernel,
        out_shape=(shape, shape),
        in_specs=[pl.BlockSpec(memory_space=pltpu.SMEM), vm, vm, hbm, hbm, hbm, hbm, vm, vm, vm, vm],
        out_specs=(vm, vm),
        scratch_shapes=[
            pltpu.VMEM((ROWS, HEAD), F32),
            pltpu.VMEM((ROWS, HEAD), F32),
            pltpu.VMEM((4, WIDTH, FEAT + 2 * HEAD), BF16),
            pltpu.VMEM((4, FEAT, WIDTH), BF16),
            pltpu.VMEM((3, ROWS, WIDTH), BF16),
            pltpu.VMEM((3, ROWS, WIDTH), BF16),
            pltpu.VMEM((ROWS, FEAT + 2 * HEAD), F32),
            pltpu.VMEM((ROWS, FEAT), F32),
            pltpu.VMEM((HEADS, ROWS, HEAD), BF16),
            pltpu.VMEM((HEAD, HEADS * ROWS), BF16),
            pltpu.VMEM((HEADS, ROWS, HEAD), BF16),
            pltpu.VMEM((HEAD, HEADS * ROWS), BF16),
            pltpu.VMEM((CHIPS, 2, 2, HALF, 2 * HEAD), BF16),
            pltpu.VMEM((ROWS, FEAT), BF16),
            pltpu.VMEM((HEAD, HEADS * ROWS), BF16),
            pltpu.VMEM((HEAD, HEADS * ROWS), F32),
            pltpu.VMEM((1, HEADS * ROWS), F32),
            pltpu.VMEM((1, HEADS * ROWS), F32),
            pltpu.VMEM((1, HEADS * ROWS), F32),
            pltpu.VMEM((1, HEADS * ROWS), F32),
            pltpu.VMEM((2, HALF, 2 * HEAD), F32),
            pltpu.VMEM((REACH + 1, 2, HALF, 2 * HEAD), F32),
            pltpu.VMEM((REACH + 1, 2, HALF, 2 * HEAD), BF16),
            pltpu.VMEM((REACH + 1, 2, HALF, 2 * HEAD), BF16),
            pltpu.VMEM((REACH, 2, HALF, 2 * HEAD), BF16),
            pltpu.VMEM((REACH, 2, HALF, 2 * HEAD), BF16),
            pltpu.VMEM((ROWS, FEAT + 2 * HEAD), BF16),
            pltpu.VMEM((3, ROWS, WIDTH), BF16),
            pltpu.VMEM((2, ROWS, WIDTH), BF16),
            pltpu.VMEM((2, HALF, WIDTH), BF16),
            pltpu.VMEM((3, ROWS, WIDTH), BF16),
            pltpu.VMEM((2, ROWS, WIDTH), BF16),
            pltpu.VMEM((2, HALF, WIDTH), BF16),
            pltpu.VMEM((2, HALF, WIDTH), F32),
            dma((16,)),
            dma((8, 2)), dma((8, 2)),
            dma((8, 2)), dma((8, 2)),
            dma((2, 4, 4)), dma((2, 4, 4)),
            dma((REACH + 1, 2)), dma((REACH + 1, 2)),
            dma((REACH + 1, 2)), dma((REACH + 1, 2)),
            dma((REACH, 2)), dma((REACH, 2)),
            dma((3, 6)), dma((3, 6)),
        ],
        compiler_params=pltpu.CompilerParams(
            collective_id=0, has_side_effects=True, vmem_limit_bytes=60 << 20
        ),
        name="attention_block",
    )(
        doc_lengths, tokens, grad_out, w_query, w_key, value_weight, w_out,
        b_query, key_bias, value_bias, freq,
    )
    return pl.pallas_call(
        hand_over,
        out_shape=(shape, shape),
        in_specs=[vm, vm],
        out_specs=(vm, vm),
        name="hand_over",
    )(*results)


def solution(mesh):
    return jax.shard_map(
        local,
        mesh=mesh,
        in_specs=(
            P("seq", "tp"),
            P(None, "tp"),
            P("tp"),
            P(None, "tp"),
            P("tp"),
            P(None, "tp"),
            P("tp"),
            P("tp", None),
            P(),
            P("seq", "tp"),
        ),
        out_specs=(P("seq", "tp"), P("seq", "tp")),
        check_vma=False,
    )
```

```python
import functools

import jax
import jax.numpy as jnp
import numpy as np
from jax import lax
from jax.experimental import pallas as pl
from jax.experimental.pallas import tpu as pltpu
from jax.sharding import PartitionSpec as P

theta_base = 1000000.0
neg_large = -1e30
log2e = 1.4426950408889634
HEAD = 128
ROWS = 256
HALF = 128
CHUNK = 64
HEADS = 5
WIDTH = 1280
FEAT = HEADS * HEAD
CHIPS = 16
REACH = 8
F32 = jnp.float32
BF16 = jnp.bfloat16
MESH = pl.DeviceIdType.MESH
factor = HEAD**-0.5
scale = factor * log2e


def nn(a, b):
    return lax.dot_general(a, b, (((1,), (0,)), ((), ())), preferred_element_type=F32)


def nt(a, b):
    return lax.dot_general(a, b, (((1,), (1,)), ((), ())), preferred_element_type=F32)


def block_kernel(
    lengths, tok, grad, wq_hbm, wk_hbm, wv_hbm, wo_hbm, bq, bk, bv, freq_ref,
    out_ref, gtok_ref,
    cos_ref, sin_ref, w, wo, tk, gr, acc, gacc, qn, qt, gn, gt, kv, at, att, oacc, m_s, l_s, lse, delta,
    tmp, own, sib_out, sib_in, dkv_out, dkv_in, x, p_out, v_out, f_out, p_grad, v_grad, f_grad, kept,
    wsem, ys, yr, fs, fr, kvs, kvr, sbs, sbr, dss, dsr, dos, dor, rss, rsr,
):
    s = lax.axis_index("seq")
    t = lax.axis_index("tp")
    chip, core = lax.div(s, 2), lax.rem(s, 2)
    right, left, opp = lax.rem(t + 1, 4), lax.rem(t + 3, 4), lax.rem(t + 2, 4)
    to_right, to_left = {"seq": s, "tp": right}, {"seq": s, "tp": left}
    sibling = {"seq": s + 1 - 2 * core, "tp": t}
    at_z, at_x = lax.div(chip, 4), lax.rem(chip, 4)
    m1 = at_x + core * (at_z - at_x)
    m2 = at_z + core * (at_x - at_z)
    stride1, stride2 = 1 + 3 * core, 4 - 3 * core

    def place(r2, r1):
        return lax.rem(m1 + 4 - r1, 4) * stride1 + lax.rem(m2 + 4 - r2, 4) * stride2

    def towards(step2, step1):
        return {"seq": 2 * place(-step2, -step1) + core, "tp": t}

    up1, down1, up2, down2 = towards(0, 1), towards(0, -1), towards(1, 0), towards(-1, 0)
    across1 = towards(0, 2)

    def remote(src, dst, send, recv, device):
        return pltpu.make_async_remote_copy(
            src_ref=src, dst_ref=dst, send_sem=send, recv_sem=recv,
            device_id=device, device_id_type=MESH,
        )

    loads = []
    for i in range(4):
        for j, (ref, lo, hi) in enumerate(
            ((wq_hbm, 0, FEAT), (wk_hbm, FEAT, FEAT + HEAD), (wv_hbm, FEAT + HEAD, FEAT + 2 * HEAD))
        ):
            loads.append(
                pltpu.make_async_copy(
                    ref.at[pl.ds(i * WIDTH, WIDTH)], w.at[i, :, lo:hi], wsem.at[3 * i + j]
                )
            )
    loads_out = [
        pltpu.make_async_copy(wo_hbm.at[:, pl.ds(i * WIDTH, WIDTH)], wo.at[i], wsem.at[12 + i])
        for i in range(4)
    ]
    for copy in loads + loads_out:
        copy.start()

    barrier = pltpu.get_barrier_semaphore()
    partners = (to_right, to_left, sibling, up1, down1, up2, down2, across1)
    for device in partners:
        pl.semaphore_signal(barrier, inc=1, device_id=device, device_id_type=MESH)
    for d in range(1, REACH + 1):
        @pl.when(chip + d < CHIPS)
        def _():
            pl.semaphore_signal(
                barrier, inc=1, device_id={"seq": s + 2 * d, "tp": t}, device_id_type=MESH
            )

        @pl.when(chip >= d)
        def _():
            pl.semaphore_signal(
                barrier, inc=1, device_id={"seq": s - 2 * d, "tp": t}, device_id_type=MESH
            )
    pl.semaphore_wait(
        barrier,
        len(partners) + jnp.minimum(chip, REACH) + jnp.minimum(CHIPS - 1 - chip, REACH),
    )

    def unit(u):
        src, buf = (tok, tk) if u < 4 else (grad, gr)
        return src, buf, pl.ds((u % 4) * CHUNK, CHUNK)

    def send(u, way):
        src, buf, sl = unit(u)
        if way == 0:
            return remote(src.at[sl], buf.at[0, sl], ys.at[u, 0], yr.at[u, 0], to_right)
        return remote(src.at[sl], buf.at[2, sl], ys.at[u, 1], yr.at[u, 1], to_left)

    def forward(u, way):
        _, buf, _ = unit(u)
        sl = pl.ds((u % 4) * CHUNK + way * (CHUNK // 2), CHUNK // 2)
        return remote(
            buf.at[2 * way, sl], buf.at[1, sl], fs.at[u, way], fr.at[u, way],
            to_left if way else to_right,
        )

    def issue(u):
        for way in range(2):
            send(u, way).start()

    def pump(u):
        for way in range(2):
            send(u, way).wait_recv()
            forward(u, way).start()

    def passed(u):
        for way in range(2):
            forward(u, way).wait_recv()

    def kv_copy(hf, r2, r1):
        if r2 == 0:
            src = (0, 0)
            device = (up1, across1, down1)[r1 - 1]
        elif r2 == 2:
            src, device = ((1, r1), up2) if r1 < 2 else ((3, r1), down2)
        else:
            src, device = (0, r1), up2 if r2 == 1 else down2
        here = kv.at[place(*src), core, hf]
        return remote(here, here, kvs.at[hf, r2, r1], kvr.at[hf, r2, r1], device)

    def kv_start(hf, *slots):
        for slot in slots:
            kv_copy(hf, *slot).start()

    def kv_wait(hf, *slots):
        for r2, r1 in slots:
            there = kv.at[place(r2, r1), core, hf]
            remote(there, there, kvs.at[hf, r2, r1], kvr.at[hf, r2, r1], sibling).wait_recv()

    def kv_second(hf):
        kv_wait(hf, (1, 0))
        kv_start(hf, (2, 0))
        for r1 in (1, 3, 2):
            kv_wait(hf, (0, r1))
            kv_start(hf, (1, r1), (3, r1))

    def kv_third(hf):
        kv_wait(hf, (1, 1))
        kv_start(hf, (2, 1))
        kv_wait(hf, (3, 3))
        kv_start(hf, (2, 3))
        kv_wait(hf, (3, 2))
        kv_start(hf, (2, 2))

    relayed = ((0, 1), (0, 2), (0, 3), (1, 0), (1, 1), (3, 2), (3, 3))

    def kv_need(hf, *distances):
        for d in distances:
            @pl.when(chip >= d)
            def _():
                back_z = at_z - lax.div(chip - d, 4)
                back_x = lax.rem(at_x + 4 - lax.rem(chip - d, 4), 4)
                r1 = back_x + core * (back_z - back_x)
                r2 = back_z + core * (back_x - back_z)
                waited = (r2 == 0) | ((r2 == 1) & (r1 < 2)) | ((r2 == 3) & (r1 >= 2))

                @pl.when(jnp.logical_not(waited))
                def _():
                    kv_wait(hf, (r2, r1))

                kv_sibling(d, hf).start()

    def kv_sibling(d, hf):
        there = kv.at[chip - d, core, hf]
        return remote(there, there, sbs.at[d, hf], sbr.at[d, hf], sibling)

    def make_rows(hf):
        sl = pl.ds(hf * HALF, HALF)
        cos, sin = cos_ref[sl, :], sin_ref[sl, :]

        def rotated(i):
            u = acc[sl, i * HEAD : (i + 1) * HEAD]
            u = u + (bq[i * HEAD : (i + 1) * HEAD] if i < HEADS else bk[...]).astype(F32)
            return (u * cos + pltpu.roll(u, HEAD // 2, 1) * sin).astype(BF16)

        kv[chip, core, hf, :, :HEAD] = rotated(HEADS)
        kv[chip, core, hf, :, HEAD:] = (
            acc[sl, (HEADS + 1) * HEAD :] + bv[...].astype(F32)
        ).astype(BF16)
        kv_start(hf, (0, 1), (0, 3), (1, 0), (3, 0), (0, 2))
        kv_sibling(0, hf).start()
        for h in range(HEADS):
            q = rotated(h)
            qn[h, sl, :] = q
            qt[:, pl.ds(h * ROWS + hf * HALF, HALF)] = q.T

    for u in range(4):
        issue(u)
    end0 = lengths[0]
    end1 = end0 + lengths[1]
    end2 = end1 + lengths[2]

    def start_at(index):
        later = jnp.where(index >= end2, end2, jnp.where(index >= end1, end1, end0))
        return jnp.where(index >= end0, later, 0)

    row_index = s * ROWS + lax.broadcasted_iota(jnp.int32, (1, ROWS), 1)
    first_key = start_at(row_index)
    index = s * ROWS + lax.broadcasted_iota(jnp.int32, (ROWS, HEAD), 0)
    angles = (index - start_at(index)).astype(F32) * freq_ref[...]
    cos_ref[...] = jnp.cos(angles)
    sine = jnp.sin(angles)
    lane = lax.broadcasted_iota(jnp.int32, (ROWS, HEAD), 1)
    sin_ref[...] = jnp.where(lane < HEAD // 2, -sine, sine)

    for copy in loads:
        copy.wait()
    acc[...] = nn(tok[...], w[t])
    pump(0)
    for copy in loads_out:
        copy.wait()
    gacc[...] = nt(grad[...], wo[t])
    m_s[...] = jnp.full(m_s.shape, neg_large, F32)
    l_s[...] = jnp.zeros(l_s.shape, F32)
    oacc[...] = jnp.zeros(oacc.shape, F32)
    pump(1)
    halves = [pl.ds(hf * HALF, HALF) for hf in range(2)]
    for hf, sl in enumerate(halves):
        if hf == 1:
            pump(2)
            pump(3)
            for u in range(4, 7):
                issue(u)
        acc[sl, :] += nn(tk[0, sl, :], w[left])
        acc[sl, :] += nn(tk[2, sl, :], w[right])
    for hf, sl in enumerate(halves):
        for u in (2 * hf, 2 * hf + 1):
            passed(u)
        acc[sl, :] += nn(tk[1, sl, :], w[opp])
        make_rows(hf)

    r2 = lax.broadcasted_iota(jnp.int32, (2 * HALF, ROWS), 0)
    key_at = jnp.where(r2 >= HALF, r2 + HALF, r2)

    def attend(first, second):
        both = jnp.concatenate(
            [
                kv[jnp.where(c < 0, chip, c), :, hf].reshape(2 * HALF, 2 * HEAD)
                for c, hf in (first, second)
            ],
            axis=0,
        )
        k = both[:, :HEAD]
        vt = both[:, HEAD:].T
        key = jnp.concatenate(
            [key_at + (c * (4 * HALF) + hf * HALF) for c, hf in (first, second)], axis=0
        )
        allowed = (key >= first_key) & (key <= row_index)
        following = nn(k, qt[:, :ROWS])
        held = None
        for h in range(HEADS + 1):
            sl = slice(h * ROWS, (h + 1) * ROWS)
            raw = following
            if h + 1 < HEADS:
                following = nn(k, qt[:, (h + 1) * ROWS : (h + 2) * ROWS])
            if held is not None:
                cols, weights, shrink = held
                oacc[:, cols] = oacc[:, cols] * shrink + nn(vt, weights)
            if h < HEADS:
                scores = jnp.where(allowed, raw * scale, neg_large)
                old = m_s[:, sl]
                top = jnp.maximum(old, jnp.max(scores, axis=0, keepdims=True))
                weights = jnp.exp2(scores - top)
                shrink = jnp.exp2(old - top)
                l_s[:, sl] = l_s[:, sl] * shrink + jnp.sum(weights, axis=0, keepdims=True)
                m_s[:, sl] = top
                held = (sl, weights.astype(BF16), shrink)

    near = ((4, 1), (3, 8), (5, 2), (7, 6))

    def pick(j, e):
        values = [pair[e] for pair in near]
        return jnp.where(
            j == 0, values[0], jnp.where(j == 1, values[1], jnp.where(j == 2, values[2], values[3]))
        )

    def forward_step(i, carry):
        j, hf = lax.rem(i + 3, 4), lax.div(i + 3, 4) - 1
        is_own = i == 0
        ahead = (pick(j, 0), pick(j, 1))

        @pl.when(i == 1)
        def _():
            kv_third(0)
            kv_need(0, *near[0], *near[1])
            kv_second(1)
            pump(4)

        @pl.when(i == 2)
        def _():
            pump(5)

        @pl.when(i == 3)
        def _():
            kv_need(0, *near[2], *near[3])

        @pl.when(i == 4)
        def _():
            kv_third(1)
            kv_need(1, *near[0], *near[1])
            pump(6)

        @pl.when(i == 5)
        def _():
            pump(7)

        @pl.when(i == 6)
        def _():
            kv_need(1, *near[2], *near[3])

        for d in ahead:
            @pl.when((i > 0) & (chip >= d))
            def _():
                kv_sibling(d, hf).wait_recv()

        @pl.when(is_own | (chip >= jnp.minimum(*ahead)))
        def _():
            attend(
                (jnp.where(is_own, chip, chip - ahead[0]), jnp.where(is_own, 0, hf)),
                (jnp.where(is_own, chip, chip - ahead[1]), jnp.where(is_own, 1, hf)),
            )

        return carry

    issue(7)
    kv_second(0)
    for hf in range(2):
        kv_sibling(0, hf).wait_recv()
    lax.fori_loop(0, REACH + 1, forward_step, 0)
    for h in range(HEADS):
        sl = slice(h * ROWS, (h + 1) * ROWS)
        mass = l_s[:, sl]
        o = (oacc[:, sl] / mass).astype(BF16)
        att[:, sl] = o
        at[:, h * HEAD : (h + 1) * HEAD] = o.T
        lse[:, sl] = m_s[:, sl] + jnp.log2(mass)

    def pieces(n):
        return ((0, HALF), (HALF, HALF)) if n == 0 else (
            ((n - 1) * HALF, CHUNK), ((n - 1) * HALF + CHUNK, CHUNK)
        )

    def passing_rows(n):
        return pl.ds(0, HALF) if n == 0 else pl.ds((n - 1) * CHUNK, CHUNK)

    def scatter_copy(i, part, arrived, passing, n):
        a, b = [pl.ds(*piece) for piece in pieces(n)]
        over = passing_rows(n)
        src, dst, device = (
            (part.at[1, a], passing.at[0, over], to_right),
            (part.at[1, b], passing.at[1, over], to_left),
            (part.at[2, b], arrived.at[0, b], to_right),
            (part.at[0, a], arrived.at[1, a], to_left),
            (part.at[2, a], arrived.at[0, a], to_right),
            (part.at[0, b], arrived.at[1, b], to_left),
        )[i]
        return remote(src, dst, rss.at[n, i], rsr.at[n, i], device)

    def scatter_early(share, part, arrived, passing, n):
        (first, rows), (second, _) = pieces(n)
        both = pl.ds(first, 2 * rows)
        part[1, both, :] = share(opp, both).astype(BF16)
        for i in range(2):
            scatter_copy(i, part, arrived, passing, n).start()
        mine = share(right, both)
        part[2, pl.ds(second, rows), :] = mine[rows:].astype(BF16)
        scatter_copy(2, part, arrived, passing, n).start()
        kept[0, pl.ds(0, rows), :] = mine[:rows]
        mine = share(left, both)
        part[0, pl.ds(first, rows), :] = mine[:rows].astype(BF16)
        scatter_copy(3, part, arrived, passing, n).start()
        kept[1, pl.ds(0, rows), :] = mine[rows:]

    def scatter_late(part, arrived, passing, n):
        for i, rel in ((0, 2), (1, 0)):
            base, rows = pieces(n)[i]
            scatter_copy(i, part, arrived, passing, n).wait_recv()
            part[rel, pl.ds(base, rows), :] = (
                kept[i, pl.ds(0, rows), :] + passing[i, passing_rows(n), :].astype(F32)
            ).astype(BF16)
            scatter_copy(4 + i, part, arrived, passing, n).start()

    def scatter_end(share, part, arrived, passing, n, result):
        (first, rows), _ = pieces(n)
        both = pl.ds(first, 2 * rows)
        mine = share(t, both)
        for i in range(2, 6):
            scatter_copy(i, part, arrived, passing, n).wait_recv()
        result[both, :] = (
            mine + arrived[0, both, :].astype(F32) + arrived[1, both, :].astype(F32)
        ).astype(BF16)
        for i in range(6):
            scatter_copy(i, part, arrived, passing, n).wait_send()

    def out_share(slot, sl):
        return nn(at[sl, :], wo[slot])

    scatter_early(out_share, p_out, v_out, f_out, 0)

    for u in range(4, 8):
        passed(u)
    g = gacc[...] + nt(gr[0], wo[left])
    g = g + nt(gr[2], wo[right])
    g = (g + nt(gr[1], wo[opp])).astype(BF16)
    for h in range(HEADS):
        part = g[:, h * HEAD : (h + 1) * HEAD]
        gn[h] = part
        gt[:, h * ROWS : (h + 1) * ROWS] = part.T
    delta[...] = jnp.sum(gt[...].astype(F32) * att[...].astype(F32), axis=0, keepdims=True)
    oacc[...] = jnp.zeros(oacc.shape, F32)

    def dkv_sibling(d, hf):
        return remote(sib_out.at[d, hf], sib_in.at[d, hf], dss.at[d, hf], dsr.at[d, hf], sibling)

    def dkv_send(d, hf):
        return remote(
            dkv_out.at[d - 1, hf], dkv_in.at[d - 1, hf], dos.at[d - 1, hf], dor.at[d - 1, hf],
            {"seq": s - 2 * d, "tp": t},
        )

    def backward(d, hf):
        both = kv[chip - d, :, hf].reshape(2 * HALF, 2 * HEAD)
        k, v = both[:, :HEAD], both[:, HEAD:]
        kt = k.T
        key = key_at + ((chip - d) * (4 * HALF) + hf * HALF)
        allowed = (key >= first_key) & (key <= row_index)
        following = (nn(k, qt[:, :ROWS]), nn(v, gt[:, :ROWS]))
        held = None
        dk = jnp.zeros((2 * HALF, HEAD), F32)
        dv = jnp.zeros((2 * HALF, HEAD), F32)
        for h in range(HEADS + 1):
            sl = slice(h * ROWS, (h + 1) * ROWS)
            raw, dprob = following
            if h + 1 < HEADS:
                nxt = slice((h + 1) * ROWS, (h + 2) * ROWS)
                following = (nn(k, qt[:, nxt]), nn(v, gt[:, nxt]))
            if held is not None:
                cols, prob_b, ds_b = held
                dv = dv + nn(prob_b, gn[h - 1])
                dk = dk + nn(ds_b, qn[h - 1])
                oacc[:, cols] = oacc[:, cols] + nn(kt, ds_b)
            if h < HEADS:
                prob = jnp.where(allowed, jnp.exp2(raw * scale - lse[:, sl]), 0.0)
                ds = prob * (dprob - delta[:, sl])
                held = (sl, prob.astype(BF16), ds.astype(BF16))
        tmp[:, :, :HEAD] = (dk * factor).reshape(2, HALF, HEAD)
        tmp[:, :, HEAD:] = dv.reshape(2, HALF, HEAD)
        own[d, hf] = tmp[core]
        sib_out[d, hf] = tmp[1 - core].astype(BF16)
        dkv_sibling(d, hf).start()

    span = REACH + 1

    def dkv_pump(i):
        d, hf = REACH - lax.rem(i, span), lax.div(i, span)

        @pl.when((chip >= d) & (d > 0))
        def _():
            dkv_sibling(d, hf).wait_recv()
            dkv_out[d - 1, hf] = (own[d, hf] + sib_in[d, hf].astype(F32)).astype(BF16)
            dkv_send(d, hf).start()

    def backward_step(i, carry):
        d, hf = REACH - lax.rem(i, span), lax.div(i, span)

        @pl.when(chip >= d)
        def _():
            backward(d, hf)

        @pl.when(i > 0)
        def _():
            dkv_pump(i - 1)

        @pl.when(i == span - 2)
        def _():
            scatter_late(p_out, v_out, f_out, 0)

        return carry

    lax.fori_loop(0, 2 * span, backward_step, 0)
    def query_rows(hf):
        sl = halves[hf]
        for h in range(HEADS):
            u = oacc[:, pl.ds(h * ROWS + hf * HALF, HALF)].T * factor
            x[sl, h * HEAD : (h + 1) * HEAD] = (
                u * cos_ref[sl, :] - pltpu.roll(u, HEAD // 2, 1) * sin_ref[sl, :]
            ).astype(BF16)

    def finish_pair(hf):
        dkv_sibling(0, hf).wait_recv()
        own[0, hf] = own[0, hf] + sib_in[0, hf].astype(F32)
        for d in range(1, REACH + 1):
            @pl.when(chip + d < CHIPS)
            def _():
                dkv_send(d, hf).wait_recv()
                own[0, hf] = own[0, hf] + dkv_in[d - 1, hf].astype(F32)
        sl = pl.ds(hf * HALF, HALF)
        u = own[0, hf, :, :HEAD]
        x[sl, FEAT : FEAT + HEAD] = (
            u * cos_ref[sl, :] - pltpu.roll(u, HEAD // 2, 1) * sin_ref[sl, :]
        ).astype(BF16)
        x[sl, FEAT + HEAD :] = own[0, hf, :, HEAD:].astype(BF16)

    def grad_share(slot, sl):
        return nt(x[sl, :], w[slot])

    query_rows(0)
    finish_pair(0)
    scatter_early(grad_share, p_grad, v_grad, f_grad, 1)
    query_rows(1)
    scatter_end(out_share, p_out, v_out, f_out, 0, out_ref)
    scatter_late(p_grad, v_grad, f_grad, 1)
    finish_pair(1)
    scatter_early(grad_share, p_grad, v_grad, f_grad, 2)
    scatter_end(grad_share, p_grad, v_grad, f_grad, 1, gtok_ref)
    scatter_late(p_grad, v_grad, f_grad, 2)

    for u in range(8):
        for way in range(2):
            send(u, way).wait_send()
            forward(u, way).wait_send()
    for hf in range(2):
        for j in range(1, 16):
            slot = (j // 4, j % 4)
            kv_copy(hf, *slot).wait_send()
            if slot not in relayed:
                gap = chip - place(*slot)

                @pl.when((gap < 1) | (gap > REACH))
                def _():
                    kv_wait(hf, slot)
        for d in range(REACH + 1):
            @pl.when(chip >= d)
            def _():
                kv_sibling(d, hf).wait_send()
                dkv_sibling(d, hf).wait_send()
                if d > 0:
                    dkv_send(d, hf).wait_send()
    scatter_end(grad_share, p_grad, v_grad, f_grad, 2, gtok_ref)


def hand_over(a, b, c, d, held, came, left):
    chunks = [
        (i, j, pl.ds(j * CHUNK, CHUNK)) for j in range(ROWS // CHUNK) for i in range(2)
    ]
    arrive = [
        pltpu.make_async_copy((a, b)[i].at[sl], held.at[i, sl], came.at[i, j]) for i, j, sl in chunks
    ]
    depart = [
        pltpu.make_async_copy(held.at[i, sl], (c, d)[i].at[sl], left.at[i, j]) for i, j, sl in chunks
    ]
    for copy in arrive:
        copy.start()
    for before, after in zip(arrive, depart):
        before.wait()
        after.start()
    for copy in depart:
        copy.wait()


def local(
    tokens, w_query, b_query, w_key, key_bias, value_weight, value_bias, w_out, doc_lengths, grad_out
):
    freq = theta_base ** (-2.0 * np.arange(HEAD // 2) / HEAD)
    freq = jnp.asarray(np.concatenate([freq, freq])[None, :], F32)
    vm = pl.BlockSpec(memory_space=pltpu.VMEM)
    hbm = pl.BlockSpec(memory_space=pl.ANY)
    dma = pltpu.SemaphoreType.DMA
    shape = jax.ShapeDtypeStruct((ROWS, WIDTH), BF16)
    results = pl.pallas_call(
        block_kernel,
        out_shape=(shape, shape),
        in_specs=[pl.BlockSpec(memory_space=pltpu.SMEM), vm, vm, hbm, hbm, hbm, hbm, vm, vm, vm, vm],
        out_specs=(vm, vm),
        scratch_shapes=[
            pltpu.VMEM((ROWS, HEAD), F32),
            pltpu.VMEM((ROWS, HEAD), F32),
            pltpu.VMEM((4, WIDTH, FEAT + 2 * HEAD), BF16),
            pltpu.VMEM((4, FEAT, WIDTH), BF16),
            pltpu.VMEM((3, ROWS, WIDTH), BF16),
            pltpu.VMEM((3, ROWS, WIDTH), BF16),
            pltpu.VMEM((ROWS, FEAT + 2 * HEAD), F32),
            pltpu.VMEM((ROWS, FEAT), F32),
            pltpu.VMEM((HEADS, ROWS, HEAD), BF16),
            pltpu.VMEM((HEAD, HEADS * ROWS), BF16),
            pltpu.VMEM((HEADS, ROWS, HEAD), BF16),
            pltpu.VMEM((HEAD, HEADS * ROWS), BF16),
            pltpu.VMEM((CHIPS, 2, 2, HALF, 2 * HEAD), BF16),
            pltpu.VMEM((ROWS, FEAT), BF16),
            pltpu.VMEM((HEAD, HEADS * ROWS), BF16),
            pltpu.VMEM((HEAD, HEADS * ROWS), F32),
            pltpu.VMEM((1, HEADS * ROWS), F32),
            pltpu.VMEM((1, HEADS * ROWS), F32),
            pltpu.VMEM((1, HEADS * ROWS), F32),
            pltpu.VMEM((1, HEADS * ROWS), F32),
            pltpu.VMEM((2, HALF, 2 * HEAD), F32),
            pltpu.VMEM((REACH + 1, 2, HALF, 2 * HEAD), F32),
            pltpu.VMEM((REACH + 1, 2, HALF, 2 * HEAD), BF16),
            pltpu.VMEM((REACH + 1, 2, HALF, 2 * HEAD), BF16),
            pltpu.VMEM((REACH, 2, HALF, 2 * HEAD), BF16),
            pltpu.VMEM((REACH, 2, HALF, 2 * HEAD), BF16),
            pltpu.VMEM((ROWS, FEAT + 2 * HEAD), BF16),
            pltpu.VMEM((3, ROWS, WIDTH), BF16),
            pltpu.VMEM((2, ROWS, WIDTH), BF16),
            pltpu.VMEM((2, HALF, WIDTH), BF16),
            pltpu.VMEM((3, ROWS, WIDTH), BF16),
            pltpu.VMEM((2, ROWS, WIDTH), BF16),
            pltpu.VMEM((2, HALF, WIDTH), BF16),
            pltpu.VMEM((2, HALF, WIDTH), F32),
            dma((16,)),
            dma((8, 2)), dma((8, 2)),
            dma((8, 2)), dma((8, 2)),
            dma((2, 4, 4)), dma((2, 4, 4)),
            dma((REACH + 1, 2)), dma((REACH + 1, 2)),
            dma((REACH + 1, 2)), dma((REACH + 1, 2)),
            dma((REACH, 2)), dma((REACH, 2)),
            dma((3, 6)), dma((3, 6)),
        ],
        compiler_params=pltpu.CompilerParams(
            collective_id=0, has_side_effects=True, vmem_limit_bytes=60 << 20
        ),
        name="attention_block",
    )(
        doc_lengths, tokens, grad_out, w_query, w_key, value_weight, w_out,
        b_query, key_bias, value_bias, freq,
    )
    return pl.pallas_call(
        hand_over,
        out_shape=(shape, shape),
        in_specs=[hbm, hbm],
        out_specs=(hbm, hbm),
        scratch_shapes=[
            pltpu.VMEM((2, ROWS, WIDTH), BF16),
            dma((2, ROWS // CHUNK)),
            dma((2, ROWS // CHUNK)),
        ],
        name="hand_over",
    )(*results)


def solution(mesh):
    return jax.shard_map(
        local,
        mesh=mesh,
        in_specs=(
            P("seq", "tp"),
            P(None, "tp"),
            P("tp"),
            P(None, "tp"),
            P("tp"),
            P(None, "tp"),
            P("tp"),
            P("tp", None),
            P(),
            P("seq", "tp"),
        ),
        out_specs=(P("seq", "tp"), P("seq", "tp")),
        check_vma=False,
    )
```
